256 devices in a mesh: dp: 32 (over y, x, core), tm: 8 (over z).
Axes of the slice: x: 4, y: 4, z: 8, core: 2. Of those that a mesh axis runs over, the one named last changes fastest.
Arguments:
- queries: bfloat16 [32, 16, 64, 3072], P('dp', 'tm'), may hold values from -16 to 16, as said below
- keys: bfloat16 [32, 16, 64, 3072], P('dp', 'tm'), may hold values from -6 to 6, as said below
- values: bfloat16 [32, 16, 64, 3072], P('dp', 'tm'), may hold values from -6 to 6
- out_grad: bfloat16 [32, 16, 64, 3072], P('dp', 'tm'), may hold values from -6 to 6
- action_table: float32 [8, 3072], replicated, may hold values from -6 to 6
- lam_tokens: bfloat16 [32, 16, 64, 1024], P('dp', 'tm'), may hold values from -60 to 60, as said below
- enc_weight: bfloat16 [1024, 1024], P('dp'), may hold values from -0.1875 to 0.1875
- codebook: float32 [8, 1024], replicated, may hold values from -6 to 6
- action_codes: int32 [32, 16], P('dp', 'tm'), may hold values from 0 to 7
- episode_start: int32 [32], P('dp'), may hold values from 0 to 15
Outputs:
- attn_out: bfloat16 [32, 16, 64, 3072], P('dp', 'tm')
- grad_q: bfloat16 [32, 16, 64, 3072], P('dp', 'tm')
- grad_k: bfloat16 [32, 16, 64, 3072], P('dp', 'tm')
- grad_v: bfloat16 [32, 16, 64, 3072], P('dp', 'tm')
- grad_actions: float32 [8, 3072], replicated
- grad_codebook: float32 [8, 1024], replicated
- grad_encoder: float32 [1024, 1024], P('dp')
The draws below stay inside these ranges and needn't reach their ends.
Inputs may be any that keep to these rules, and one draw needn't show every extreme that they name: `queries`: bfloat16 activations. `keys`: bfloat16 activations. `lam_tokens`: bfloat16 tokens.
All inputs are finite; a program needn't handle non-finite values.
Results may differ from the reference program's by a relative error of at most 0.024.
Values may be sent and summed in bfloat16 or wider, within the bound.
A program may use at most 128 MiB of HBM per device.

```python
import math
import jax
import jax.numpy as jnp
from jax import lax

HS = 128
HEADS = 24
DL = 1024
NC = 8
F = 16
P_SIZE = 64
CLIPS = 32


def draw_queries(key, part):
    key = jax.random.fold_in(key, 7)
    shape = (CLIPS, F, P_SIZE, HEADS * HS)
    base = jnp.clip(jax.random.normal(key, shape, jnp.float32), -6.0, 6.0)
    return base.astype(jnp.bfloat16)


def draw_keys(key, part):
    key = jax.random.fold_in(key, 9)
    shape = (CLIPS, F, P_SIZE, HEADS * HS)
    base = jnp.clip(jax.random.normal(key, shape, jnp.float32), -6.0, 6.0)
    return base.astype(jnp.bfloat16)


def draw_lam_tokens(key, part):
    key = jax.random.fold_in(key, 5)
    shape = (CLIPS, F, P_SIZE, DL)
    base = jnp.clip(jax.random.normal(key, shape, jnp.float32), -6.0, 6.0)
    return base.astype(jnp.bfloat16)


def set_ends(entries, stream_key, low, largest):
    longest = entries.shape.index(max(entries.shape))
    spots = []
    for shift in (0, 1):
        where = [jax.random.randint(jax.random.fold_in(stream_key, axis), (), 0, length) for axis, length in enumerate(entries.shape)]
        where[longest] = (where[longest] + shift) % entries.shape[longest]
        spots.append(tuple(where))
    return entries.at[spots[0]].set(low).at[spots[1]].set(largest)


def shard_levels(key, shape, pieces, smallest, high):
    level = 1.0
    for dim, shards_of in pieces:
        steps = jax.random.uniform(jax.random.fold_in(jax.random.fold_in(key, 6), dim), (shards_of,), jnp.float32, smallest / len(pieces), high / len(pieces))
        level = level * jnp.repeat(jnp.exp(steps), shape[dim] // shards_of).reshape((-1,) + (1,) * (len(shape) - 1 - dim))
    return level


def bell_draw(key, shape, width, bound, shards=(), dtype=jnp.bfloat16):
    level = shard_levels(key, shape, shards, -0.22, 0.18) if shards else 1.0
    result = jax.random.normal(key, shape, jnp.float32) * width * level
    return jnp.minimum(jnp.maximum(result, -bound), bound).astype(dtype)


def setup_inputs(seed: int = 0) -> dict:
    key_list = jax.random.split(jax.random.key(seed), 11)
    return {
        "queries": draw_queries(jax.random.fold_in(key_list[10], 71), 0),
        "keys": draw_keys(jax.random.fold_in(key_list[10], 71), 0),
        "values": bell_draw(key_list[2], (CLIPS, F, P_SIZE, HEADS * HS), 1.0, 6.0, ((0, 32), (1, 8))),
        "out_grad": bell_draw(key_list[3], (CLIPS, F, P_SIZE, HEADS * HS), 1.0, 6.0, ((0, 32), (1, 8))),
        "action_table": bell_draw(key_list[4], (NC, HEADS * HS), 1.0, 6.0, (), jnp.float32),
        "lam_tokens": draw_lam_tokens(jax.random.fold_in(key_list[10], 71), 0),
        "enc_weight": bell_draw(key_list[6], (DL, DL), DL ** -0.5, 0.1875, ((0, 32),)),
        "codebook": bell_draw(key_list[7], (NC, DL), 1.0, 6.0, (), jnp.float32),
        "action_codes": set_ends(jax.random.randint(key_list[8], (CLIPS, F), 0, NC), jax.random.fold_in(key_list[8], 1), 0, NC - 1).astype(jnp.int32),
        "episode_start": set_ends(jax.random.randint(key_list[9], (CLIPS,), 0, F), jax.random.fold_in(key_list[9], 1), 0, F - 1).astype(jnp.int32),
    }


NEG_FILL = -1e+30

def round_bf(array):
    return lax.optimization_barrier(array.astype(jnp.bfloat16))

def clip_attention(conditioned, key_rows, value_rows, grad_rows, boundary):
    all_rows = F * P_SIZE
    frame_ids = jnp.arange(all_rows) // P_SIZE
    later = frame_ids >= boundary
    visible = (frame_ids[None, :] <= frame_ids[:, None]) & (later[None, :] == later[:, None])
    score_scale = 1.0 / math.sqrt(HS)
    query_heads = conditioned.reshape(all_rows, HEADS, HS).astype(jnp.float32)
    key_heads = key_rows.reshape(all_rows, HEADS, HS).astype(jnp.float32)
    value_heads = value_rows.reshape(all_rows, HEADS, HS).astype(jnp.float32)
    grad_heads = grad_rows.reshape(all_rows, HEADS, HS).astype(jnp.float32)
    scores = jnp.einsum('qhd,khd->hqk', query_heads, key_heads) * score_scale
    scores = jnp.where(visible[None], scores, NEG_FILL)
    row_top = lax.optimization_barrier(jnp.max(scores, axis=2, keepdims=True))
    log_total = row_top + jnp.log(lax.optimization_barrier(jnp.sum(jnp.exp(scores - row_top), axis=2, keepdims=True)))
    probability = jnp.exp(scores - log_total)
    weights = round_bf(probability).astype(jnp.float32)
    output = round_bf(jnp.einsum('hqk,khd->qhd', weights, value_heads))
    out_float = output.astype(jnp.float32)
    grad_dot = lax.optimization_barrier(jnp.sum(grad_heads * out_float, axis=2)).T[:, :, None]
    prob_grad = jnp.einsum('qhd,khd->hqk', grad_heads, value_heads)
    score_grad = round_bf(probability * (prob_grad - grad_dot) * score_scale).astype(jnp.float32)
    grad_query = jnp.einsum('hqk,khd->qhd', score_grad, key_heads).astype(jnp.bfloat16)
    grad_key = jnp.einsum('hqk,qhd->khd', score_grad, query_heads).astype(jnp.bfloat16)
    grad_value = jnp.einsum('hqk,qhd->khd', weights, grad_heads).astype(jnp.bfloat16)
    shape = (F, P_SIZE, HEADS * HS)
    return (output.reshape(shape), grad_query.reshape(shape), grad_key.reshape(shape), grad_value.reshape(shape))

def reference(queries, keys, values, out_grad, action_table, lam_tokens, enc_weight, codebook, action_codes, episode_start):
    highest = lax.Precision.HIGHEST
    onehot = (action_codes[:, :, None] == jnp.arange(NC)[None, None, :]).astype(jnp.float32)
    offsets = jnp.einsum('cfn,nd->cfd', onehot, action_table, precision=highest)
    conditioned = (queries.astype(jnp.float32) + offsets[:, :, None, :]).astype(jnp.bfloat16)
    results = lax.map(lambda packed: clip_attention(*packed), (conditioned, keys, values, out_grad, episode_start))
    attn_out, grad_q, grad_k, grad_v = results
    summed = lax.optimization_barrier(jnp.sum(grad_q.astype(jnp.float32), axis=2))
    grad_actions = jnp.einsum('cfn,cfd->nd', onehot, summed, precision=highest)
    frames_in = lam_tokens.astype(jnp.float32)
    previous = jnp.concatenate([jnp.zeros_like(frames_in[:, :1]), frames_in[:, :-1]], axis=1)
    delta = (frames_in - previous).astype(jnp.bfloat16)
    delta_rows = delta.reshape(-1, DL)
    encoded = jnp.dot(delta_rows, enc_weight, preferred_element_type=jnp.float32).reshape(CLIPS, F, P_SIZE, DL)
    pooled = lax.optimization_barrier(jnp.mean(jax.nn.silu(encoded), axis=2))
    target = jnp.einsum('cfn,nd->cfd', onehot, codebook, precision=highest)
    frame_ids = jnp.arange(F)
    live_pairs = ((frame_ids[None, :] >= 1) & (frame_ids[None, :] != episode_start[:, None])).astype(jnp.float32)
    residual = (pooled - target) * live_pairs[:, :, None] / F
    grad_codebook = -jnp.einsum('cfn,cfd->nd', onehot, residual, precision=highest)
    sigmoid_u = jax.nn.sigmoid(encoded)
    silu_slope = sigmoid_u * (1.0 + encoded * (1.0 - sigmoid_u))
    encoded_grad = ((residual / P_SIZE)[:, :, None, :] * silu_slope).astype(jnp.bfloat16).reshape(-1, DL)
    grad_encoder = lax.dot_general(delta_rows, encoded_grad, (((0,), (0,)), ((), ())), preferred_element_type=jnp.float32)
    return (attn_out, grad_q, grad_k, grad_v, grad_actions, grad_codebook, grad_encoder)
```

```python
import functools
import math

import jax
import jax.numpy as jnp
from jax import lax
from jax.experimental import pallas as pl
from jax.experimental.pallas import tpu as pltpu
from jax.sharding import PartitionSpec as P

HS = 128
NC = 8
NEG_FILL = -1e30
MESH = pl.DeviceIdType.MESH
BF = jnp.bfloat16
F32 = jnp.float32


def dot(a, b):
    return jnp.dot(a, b, preferred_element_type=F32)


def wait_bytes(view, sem):
    pltpu.make_async_copy(view, view, sem).wait()


def kernel(
    sizes,
    q_ref, k_ref, v_ref, g_ref, tab_ref, lam_ref, enc_ref, book_ref, code_ref, start_ref,
    o_out, dq_out, dk_out, dv_out, ga_out, gc_out, ge_out,
    cond, qb, kb, vb, gb, ob, dqb, dkb, dvb, kt, vt, qt, gt, dk_acc, dv_acc,
    onehot, prev, wg, dw, rc, s1, ry, s2, rx, s3, rt, s4,
    cterm, cin, blob, core_in, y_in, x_in,
    in_recv, in_send, out_recv, out_send, small_recv, small_send,
):
    ny, nx, nc, nt, chunk = sizes
    heads = qb.shape[0]
    rows = qb.shape[1]
    here = rows // nt
    per_frame = here // 2
    width = heads * HS
    lam_width = lam_ref.shape[1]
    part = lam_width // nt
    enc_rows = enc_ref.shape[0]
    dp = lax.axis_index("dp")
    me = lax.axis_index("tm")
    core = dp % nc
    xx = (dp // nc) % nx
    yy = dp // (nc * nx)

    def at_t(t):
        return (dp, t)

    def at_x(x):
        return ((yy * nx + x) * nc + core, me)

    def at_y(y):
        return ((y * nx + xx) * nc + core, me)

    other_core = ((yy * nx + xx) * nc + (nc - 1 - core), me)

    def over_t(fn):
        def body(i, carry):
            step = nt // 2 + (1 - 2 * (i % 2)) * ((i + 1) // 2)
            fn((me + step) % nt)
            return carry

        lax.fori_loop(0, nt - 1, body, 0)

    def over_x(fn):
        def body(i, carry):
            fn((xx + 1 + i) % nx)
            return carry

        lax.fori_loop(0, nx - 1, body, 0)

    def over_y(fn):
        def body(i, carry):
            fn((yy + 1 + i) % ny)
            return carry

        lax.fori_loop(0, ny - 1, body, 0)

    barrier = pltpu.get_barrier_semaphore()

    def greet(device):
        pl.semaphore_signal(barrier, inc=1, device_id=device, device_id_type=MESH)

    over_t(lambda t: greet(at_t(t)))
    over_x(lambda x: greet(at_x(x)))
    over_y(lambda y: greet(at_y(y)))
    greet(other_core)
    pl.semaphore_wait(barrier, (nt - 1) + (nx - 1) + (ny - 1) + 1)

    def send(src, dst, sem_s, sem_r, device):
        pltpu.make_async_remote_copy(
            src_ref=src, dst_ref=dst, send_sem=sem_s, recv_sem=sem_r,
            device_id=device, device_id_type=MESH,
        ).start()

    LAM, AGX, AGY, AGC, HOT, RSC, RSY, RSX, RST, GE, CT, ARC, ARY, ARX, FA, FC = range(16)

    def small(src, dst, index, device):
        send(src, dst, small_send.at[index], small_recv.at[index], device)

    def lanes(index, size):
        return pl.ds(pl.multiple_of(index * size, size), size)

    wg[yy, xx, core] = enc_ref[...]
    over_x(lambda x: small(enc_ref, wg.at[yy, xx, core], AGX, at_x(x)))
    small(lam_ref.at[pl.ds(per_frame, per_frame)], prev, LAM, at_t((me + 1) % nt))
    code_a, code_b = code_ref[0, 0], code_ref[0, 1]
    boundary = start_ref[0]
    lane_code = jnp.where(
        lax.broadcasted_iota(jnp.int32, (NC, here), 1) < per_frame, code_a, code_b
    )
    hot_here = (lax.broadcasted_iota(jnp.int32, (NC, here), 0) == lane_code).astype(F32)
    onehot[:, lanes(me, here)] = hot_here
    over_t(lambda t: small(onehot.at[:, lanes(me, here)], onehot.at[:, lanes(me, here)], HOT, at_t(t)))

    mine = pl.ds(pl.multiple_of(me * here, here), here)

    def scatter_in(index, src, dst, head):
        def one(t):
            send(
                src.at[:, lanes(t * heads + head, HS)], dst.at[head, mine],
                in_send.at[index], in_recv.at[index, head], at_t(t),
            )

        over_t(one)
        pltpu.make_async_copy(
            src.at[:, lanes(me * heads + head, HS)], dst.at[head, mine], in_recv.at[index, head]
        ).start()

    scatter_in(1, k_ref, kb, 0)
    scatter_in(2, v_ref, vb, 0)
    table = tab_ref[...]
    code_ids = lax.broadcasted_iota(jnp.int32, table.shape, 0)
    for frame, code in ((0, code_a), (1, code_b)):
        offset = jnp.sum(jnp.where(code_ids == code, table, 0.0), axis=0, keepdims=True)
        span = pl.ds(frame * per_frame, per_frame)
        cond[span] = (q_ref[span].astype(F32) + offset).astype(BF)
    scatter_in(0, cond, qb, 0)
    scatter_in(3, g_ref, gb, 0)
    for head in range(1, heads):
        scatter_in(1, k_ref, kb, head)
        scatter_in(0, cond, qb, head)
        scatter_in(2, v_ref, vb, head)
        scatter_in(3, g_ref, gb, head)

    wait_bytes(wg.at[0, pl.ds(0, nx - 1), 0], small_recv.at[AGX])
    over_y(lambda y: small(wg.at[yy, :, core], wg.at[yy, :, core], AGY, at_y(y)))
    wait_bytes(prev, small_recv.at[LAM])
    lam = lam_ref[...].astype(F32)
    before = jnp.where(me > 0, prev[...].astype(F32), 0.0)
    delta = jnp.concatenate(
        [lam[:per_frame] - before, lam[per_frame:] - lam[:per_frame]], axis=0
    ).astype(BF)
    wait_bytes(wg.at[pl.ds(0, ny - 1), :, 0], small_recv.at[AGY])
    small(wg.at[:, :, core], wg.at[:, :, core], AGC, other_core)
    delta_t = delta.T
    wait_bytes(wg.at[:, :, 0], small_recv.at[AGC])
    slab = lam_width // ny
    encoded = jnp.zeros((here, lam_width), F32)
    for y in range(ny):
        encoded += dot(delta[:, y * slab:(y + 1) * slab], wg[y].reshape(slab, lam_width))
    sig = jax.nn.sigmoid(encoded)
    act = encoded * sig
    slope = sig * (1.0 + encoded * (1.0 - sig))
    book = book_ref[...]
    book_ids = lax.broadcasted_iota(jnp.int32, book.shape, 0)
    term = jnp.zeros(book.shape, F32)
    graded = []
    for frame, code in ((0, code_a), (1, code_b)):
        span = slice(frame * per_frame, (frame + 1) * per_frame)
        pooled = jnp.sum(act[span], axis=0, keepdims=True) * (1.0 / per_frame)
        target = jnp.sum(jnp.where(book_ids == code, book, 0.0), axis=0, keepdims=True)
        frame_id = me * 2 + frame
        live = jnp.where((frame_id >= 1) & (frame_id != boundary), 1.0 / (2 * nt), 0.0)
        residual = (pooled - target) * live
        term -= jnp.where(book_ids == code, residual, 0.0)
        graded.append(residual * (1.0 / per_frame) * slope[span])
    encoded_grad = jnp.concatenate(graded, axis=0).astype(BF)
    for t in range(nt):
        cterm[t] = term[:, t * part:(t + 1) * part]
    cin[me] = cterm[me]
    over_t(lambda t: small(cterm.at[t], cin.at[me], CT, at_t(t)))
    for yx in range(ny * nx):
        lo = yx * nc * enc_rows
        piece = dot(delta_t[lo:lo + nc * enc_rows], encoded_grad).astype(BF)
        for c in range(nc):
            dw[c, yx // nx, yx % nx] = piece[c * enc_rows:(c + 1) * enc_rows]
    small(dw.at[nc - 1 - core], rc, RSC, other_core)

    def add_cores():
        wait_bytes(rc, small_recv.at[RSC])
        for y in range(ny):
            s1[y] = (dw[core, y].astype(F32) + rc[y].astype(F32)).astype(BF)
        over_y(lambda y: small(s1.at[y], ry.at[yy], RSY, at_y(y)))
        ry[yy] = s1[yy]

    def add_y():
        wait_bytes(ry.at[pl.ds(0, ny - 1)], small_recv.at[RSY])
        total = ry[0].astype(F32)
        for y in range(1, ny):
            total += ry[y].astype(F32)
        s2[...] = total.astype(BF)
        over_x(lambda x: small(s2.at[x], rx.at[xx], RSX, at_x(x)))
        rx[xx] = s2[xx]

    def add_x():
        wait_bytes(rx.at[pl.ds(0, nx - 1)], small_recv.at[RSX])
        total = rx[0].astype(F32)
        for x in range(1, nx):
            total += rx[x].astype(F32)
        total = total.astype(BF)
        for t in range(nt):
            s3[t] = total[:, t * part:(t + 1) * part]
        over_t(lambda t: small(s3.at[t], rt.at[me], RST, at_t(t)))
        rt[me] = s3[me]

    def add_t():
        wait_bytes(rt.at[pl.ds(0, nt - 1)], small_recv.at[RST])
        total = rt[0].astype(F32)
        for t in range(1, nt):
            total += rt[t].astype(F32)
        s4[...] = total.astype(BF).astype(F32)
        over_t(lambda t: small(s4, ge_out.at[:, lanes(me, part)], GE, at_t(t)))
        pltpu.make_async_copy(s4, ge_out.at[:, lanes(me, part)], small_recv.at[GE]).start()

    score_scale = 1.0 / math.sqrt(HS)
    exp_scale = score_scale * math.log2(math.e)

    def attend(head):
        for index, block in ((0, qb), (1, kb), (2, vb), (3, gb)):
            wait_bytes(block.at[head], in_recv.at[index, head])
        kt[...] = kb[head].T
        vt[...] = vb[head].T
        qt[...] = qb[head].T
        gt[...] = gb[head].T
        for c in reversed(range(rows // chunk)):
            size = (c + 1) * chunk
            span = slice(c * chunk, size)
            scores = dot(kb[head, :size], qt[:, span])
            frame_of = (lax.broadcasted_iota(jnp.int32, (1, chunk), 1) + c * chunk) // per_frame
            low = jnp.where(frame_of >= boundary, boundary, 0) * per_frame
            high = (frame_of + 1) * per_frame
            key_ids = lax.broadcasted_iota(jnp.int32, (size, chunk), 0)
            scores = jnp.where((key_ids >= low) & (key_ids < high), scores, NEG_FILL)
            top = jnp.max(scores, axis=0, keepdims=True)
            prob = jnp.exp2((scores - top) * exp_scale)
            prob = prob * (1.0 / jnp.sum(prob, axis=0, keepdims=True))
            weights = prob.astype(BF)
            out_t = dot(vt[:, :size], weights).astype(BF)
            ob[head, span] = out_t.T
            g_t = gt[:, span]
            grad_dot = jnp.sum(g_t.astype(F32) * out_t.astype(F32), axis=0, keepdims=True)
            prob_grad = dot(vb[head, :size], g_t)
            score_grad = (prob * ((prob_grad - grad_dot) * score_scale)).astype(BF)
            dqb[head, span] = dot(kt[:, :size], score_grad).astype(BF).T
            dk_part = dot(score_grad, qb[head, span])
            dv_part = dot(weights, gb[head, span])
            if size == rows:
                dk_acc[...] = dk_part
                dv_acc[...] = dv_part
            else:
                dk_acc[:size] += dk_part
                dv_acc[:size] += dv_part
        dkb[head] = dk_acc[...].astype(BF)
        dvb[head] = dv_acc[...].astype(BF)
        for index, src, dst in ((0, ob, o_out), (1, dqb, dq_out), (2, dkb, dk_out), (3, dvb, dv_out)):
            columns = lanes(me * heads + head, HS)

            def block(t):
                return src.at[head, pl.ds(pl.multiple_of(t * here, here), here)]

            over_t(lambda t: send(
                block(t), dst.at[:, columns], out_send.at[index], out_recv.at[index], at_t(t)
            ))
            pltpu.make_async_copy(block(me), dst.at[:, columns], out_recv.at[index]).start()

    def head_step(head, carry):
        attend(head)

        @pl.when(head == 0)
        def _():
            add_cores()

        @pl.when(head == 1)
        def _():
            add_y()

        return carry

    lax.fori_loop(0, heads, head_step, 0)
    add_x()

    wait_bytes(onehot.at[:, pl.ds(0, (nt - 1) * here)], small_recv.at[HOT])
    hot = onehot[...].astype(BF)
    for head in range(heads):
        blob[:, head * HS:(head + 1) * HS] = dot(hot, dqb[head])
    wait_bytes(cin.at[pl.ds(0, nt - 1)], small_recv.at[CT])
    total = cin[0]
    for t in range(1, nt):
        total += cin[t]
    blob[:, width:] = total
    small(blob, core_in, ARC, other_core)
    add_t()
    wait_bytes(core_in, small_recv.at[ARC])
    y_in[yy] = blob[...] + core_in[...]
    over_y(lambda y: small(y_in.at[yy], y_in.at[yy], ARY, at_y(y)))
    wait_bytes(y_in.at[pl.ds(0, ny - 1)], small_recv.at[ARY])
    total = y_in[0]
    for y in range(1, ny):
        total += y_in[y]
    x_in[xx] = total
    over_x(lambda x: small(x_in.at[xx], x_in.at[xx], ARX, at_x(x)))
    wait_bytes(x_in.at[pl.ds(0, nx - 1)], small_recv.at[ARX])
    total = x_in[0]
    for x in range(1, nx):
        total += x_in[x]
    wait_bytes(blob, small_send.at[ARC])
    blob[...] = total
    act_part, book_part = blob.at[:, pl.ds(0, width)], blob.at[:, pl.ds(width, part)]
    act_dst, book_dst = ga_out.at[:, lanes(me, width)], gc_out.at[:, lanes(me, part)]
    over_t(lambda t: small(act_part, act_dst, FA, at_t(t)))
    over_t(lambda t: small(book_part, book_dst, FC, at_t(t)))
    pltpu.make_async_copy(act_part, act_dst, small_recv.at[FA]).start()
    pltpu.make_async_copy(book_part, book_dst, small_recv.at[FC]).start()

    for index, dst in enumerate((o_out, dq_out, dk_out, dv_out)):
        wait_bytes(dst, out_recv.at[index])
    wait_bytes(ge_out, small_recv.at[GE])
    wait_bytes(ga_out, small_recv.at[FA])
    wait_bytes(gc_out, small_recv.at[FC])
    sent = qb.at[:, pl.ds(0, rows - here)]
    for index in range(4):
        wait_bytes(sent, in_send.at[index])
        wait_bytes(sent, out_send.at[index])
    for index, view in (
        (LAM, prev),
        (AGX, wg.at[0, pl.ds(0, nx - 1), 0]),
        (AGY, wg.at[pl.ds(0, ny - 1), :, 0]),
        (AGC, wg.at[:, :, 0]),
        (HOT, onehot.at[:, pl.ds(0, (nt - 1) * here)]),
        (RSC, rc),
        (RSY, ry.at[pl.ds(0, ny - 1)]),
        (RSX, rx.at[pl.ds(0, nx - 1)]),
        (RST, rt.at[pl.ds(0, nt - 1)]),
        (GE, ge_out.at[:, pl.ds(0, (nt - 1) * part)]),
        (CT, cin.at[pl.ds(0, nt - 1)]),
        (ARY, y_in.at[pl.ds(0, ny - 1)]),
        (ARX, x_in.at[pl.ds(0, nx - 1)]),
        (FA, ga_out.at[:, pl.ds(0, (nt - 1) * width)]),
        (FC, gc_out.at[:, pl.ds(0, (nt - 1) * part)]),
    ):
        wait_bytes(view, small_send.at[index])


def per_device(
    ny, nx, nc, nt, chunk,
    queries, keys, values, out_grad, action_table, lam_tokens, enc_weight, codebook,
    action_codes, episode_start,
):
    shape = queries.shape
    here = shape[1] * shape[2]
    wide = shape[3]
    lam_width = lam_tokens.shape[3]
    heads = wide // HS // nt
    rows = here * nt
    part = lam_width // nt
    enc_rows = enc_weight.shape[0]
    vmem = pl.BlockSpec(memory_space=pltpu.VMEM)
    smem = pl.BlockSpec(memory_space=pltpu.SMEM)
    anywhere = pl.BlockSpec(memory_space=pl.ANY)
    head_block = pltpu.VMEM((heads, rows, HS), BF)
    turned = pltpu.VMEM((HS, rows), BF)
    flops = heads * rows * rows * HS * 2 * 6 + 2 * 2 * here * lam_width * lam_width
    flat = jax.ShapeDtypeStruct((here, wide), BF)
    results = pl.pallas_call(
        functools.partial(kernel, (ny, nx, nc, nt, chunk)),
        out_shape=(
            flat, flat, flat, flat,
            jax.ShapeDtypeStruct(action_table.shape, F32),
            jax.ShapeDtypeStruct(codebook.shape, F32),
            jax.ShapeDtypeStruct(enc_weight.shape, F32),
        ),
        in_specs=[vmem, anywhere, anywhere, anywhere, vmem, vmem, vmem, vmem, smem, smem],
        out_specs=[anywhere] * 7,
        scratch_shapes=[
            pltpu.VMEM((here, wide), BF),
            head_block, head_block, head_block, head_block,
            head_block, head_block, head_block, head_block,
            turned, turned, turned, turned,
            pltpu.VMEM((rows, HS), F32),
            pltpu.VMEM((rows, HS), F32),
            pltpu.VMEM((NC, rows), F32),
            pltpu.VMEM((here // 2, lam_width), BF),
            pltpu.VMEM((ny, nx, nc, enc_rows, lam_width), BF),
            pltpu.VMEM((nc, ny, nx, enc_rows, lam_width), BF),
            pltpu.VMEM((ny, nx, enc_rows, lam_width), BF),
            pltpu.VMEM((ny, nx, enc_rows, lam_width), BF),
            pltpu.VMEM((ny, nx, enc_rows, lam_width), BF),
            pltpu.VMEM((nx, enc_rows, lam_width), BF),
            pltpu.VMEM((nx, enc_rows, lam_width), BF),
            pltpu.VMEM((nt, enc_rows, part), BF),
            pltpu.VMEM((nt, enc_rows, part), BF),
            pltpu.VMEM((enc_rows, part), F32),
            pltpu.VMEM((nt, NC, part), F32),
            pltpu.VMEM((nt, NC, part), F32),
            pltpu.VMEM((NC, heads * HS + part), F32),
            pltpu.VMEM((NC, heads * HS + part), F32),
            pltpu.VMEM((ny, NC, heads * HS + part), F32),
            pltpu.VMEM((nx, NC, heads * HS + part), F32),
            pltpu.SemaphoreType.DMA((4, heads)),
            pltpu.SemaphoreType.DMA((4,)),
            pltpu.SemaphoreType.DMA((4,)),
            pltpu.SemaphoreType.DMA((4,)),
            pltpu.SemaphoreType.DMA((16,)),
            pltpu.SemaphoreType.DMA((16,)),
        ],
        compiler_params=pltpu.CompilerParams(
            collective_id=0, has_side_effects=True, vmem_limit_bytes=56 * 2**20
        ),
        cost_estimate=pl.CostEstimate(
            flops=flops, bytes_accessed=8 * here * wide * 2, transcendentals=heads * rows * rows
        ),
    )(
        queries.reshape(here, wide), keys.reshape(here, wide), values.reshape(here, wide),
        out_grad.reshape(here, wide), action_table, lam_tokens.reshape(here, lam_width),
        enc_weight, codebook, action_codes, episode_start,
    )
    return tuple(r.reshape(shape) for r in results[:4]) + tuple(results[4:])


def solution(mesh, dims=(4, 4, 2), chunk=256):
    ny, nx, nc = dims
    nt = mesh.shape["tm"]
    frames = P("dp", "tm", None, None)
    return jax.shard_map(
        functools.partial(per_device, ny, nx, nc, nt, chunk),
        mesh=mesh,
        in_specs=(
            frames, frames, frames, frames, P(), frames, P("dp", None), P(), P("dp", "tm"), P("dp"),
        ),
        out_specs=(frames, frames, frames, frames, P(), P(), P("dp", None)),
        check_vma=False,
    )
```

```python
import functools
import math

import jax
import jax.numpy as jnp
from jax import lax
from jax.experimental import pallas as pl
from jax.experimental.pallas import tpu as pltpu
from jax.sharding import PartitionSpec as P

HS = 128
NC = 8
NEG_FILL = -1e30
MESH = pl.DeviceIdType.MESH
BF = jnp.bfloat16
F32 = jnp.float32


def dot(a, b):
    return jnp.dot(a, b, preferred_element_type=F32)


def wait_bytes(view, sem):
    pltpu.make_async_copy(view, view, sem).wait()


def kernel(
    sizes,
    q_hbm, k_ref, v_ref, g_ref, tab_hbm, lam_hbm, enc_hbm, book_hbm, code_ref, start_ref,
    o_out, dq_out, dk_out, dv_out, ga_out, gc_out, ge_out,
    q_ref, tab_ref, lam_ref, book_ref, cond, qb, kb, vb, gb, ob, dqb, dkb, dvb, kt, vt, qt, gt, dk_acc, dv_acc,
    onehot, prev, wg, dw, rc, s1, ry, s2, rx, s3, rt, s4, ge,
    cterm, cin, blob, core_in, y_in, x_in,
    load, in_recv, in_send, out_recv, out_send, small_recv, small_send,
):
    ny, nx, nc, nt, chunk = sizes
    heads = qb.shape[0]
    rows = qb.shape[1]
    here = rows // nt
    per_frame = here // 2
    width = heads * HS
    lam_width = lam_ref.shape[1]
    part = lam_width // nt
    enc_rows = enc_hbm.shape[0]
    dp = lax.axis_index("dp")
    me = lax.axis_index("tm")
    core = dp % nc
    xx = (dp // nc) % nx
    yy = dp // (nc * nx)

    def at_t(t):
        return (dp, t)

    def at_x(x):
        return ((yy * nx + x) * nc + core, me)

    def at_y(y):
        return ((y * nx + xx) * nc + core, me)

    other_core = ((yy * nx + xx) * nc + (nc - 1 - core), me)

    def over_t(fn):
        def body(i, carry):
            step = nt // 2 + (1 - 2 * (i % 2)) * ((i + 1) // 2)
            fn((me + step) % nt)
            return carry

        lax.fori_loop(0, nt - 1, body, 0)

    def over_x(fn):
        def body(i, carry):
            fn((xx + 1 + i) % nx)
            return carry

        lax.fori_loop(0, nx - 1, body, 0)

    def over_y(fn):
        def body(i, carry):
            fn((yy + 1 + i) % ny)
            return carry

        lax.fori_loop(0, ny - 1, body, 0)

    own_rows = wg.at[yy, xx, core]
    loads = [
        pltpu.make_async_copy(src, dst, load.at[i])
        for i, (src, dst) in enumerate((
            (enc_hbm, own_rows), (lam_hbm, lam_ref), (q_hbm, q_ref),
            (tab_hbm, tab_ref), (book_hbm, book_ref),
        ))
    ]
    for copy in loads:
        copy.start()

    barrier = pltpu.get_barrier_semaphore()

    def greet(device):
        pl.semaphore_signal(barrier, inc=1, device_id=device, device_id_type=MESH)

    over_t(lambda t: greet(at_t(t)))
    over_x(lambda x: greet(at_x(x)))
    over_y(lambda y: greet(at_y(y)))
    greet(other_core)
    pl.semaphore_wait(barrier, (nt - 1) + (nx - 1) + (ny - 1) + 1)

    def send(src, dst, sem_s, sem_r, device):
        pltpu.make_async_remote_copy(
            src_ref=src, dst_ref=dst, send_sem=sem_s, recv_sem=sem_r,
            device_id=device, device_id_type=MESH,
        ).start()

    LAM, AGX, AGY, AGC, HOT, RSC, RSY, RSX, RST, GE, CT, ARC, ARY, ARX, FA, FC = range(16)

    def small(src, dst, index, device):
        send(src, dst, small_send.at[index], small_recv.at[index], device)

    def lanes(index, size):
        return pl.ds(pl.multiple_of(index * size, size), size)

    loads[0].wait()
    over_x(lambda x: small(own_rows, own_rows, AGX, at_x(x)))
    loads[1].wait()
    small(lam_ref.at[pl.ds(per_frame, per_frame)], prev, LAM, at_t((me + 1) % nt))
    code_a, code_b = code_ref[0, 0], code_ref[0, 1]
    boundary = start_ref[0]
    lane_code = jnp.where(
        lax.broadcasted_iota(jnp.int32, (NC, here), 1) < per_frame, code_a, code_b
    )
    hot_here = (lax.broadcasted_iota(jnp.int32, (NC, here), 0) == lane_code).astype(F32)
    onehot[:, lanes(me, here)] = hot_here
    over_t(lambda t: small(onehot.at[:, lanes(me, here)], onehot.at[:, lanes(me, here)], HOT, at_t(t)))

    mine = pl.ds(pl.multiple_of(me * here, here), here)

    def scatter_in(index, src, dst, head):
        def one(t):
            send(
                src.at[:, lanes(t * heads + head, HS)], dst.at[head, mine],
                in_send.at[index], in_recv.at[index, head], at_t(t),
            )

        over_t(one)
        pltpu.make_async_copy(
            src.at[:, lanes(me * heads + head, HS)], dst.at[head, mine], in_recv.at[index, head]
        ).start()

    scatter_in(1, k_ref, kb, 0)
    for copy in loads[2:]:
        copy.wait()
    table = tab_ref[...]
    code_ids = lax.broadcasted_iota(jnp.int32, table.shape, 0)
    for frame, code in ((0, code_a), (1, code_b)):
        offset = jnp.sum(jnp.where(code_ids == code, table, 0.0), axis=0, keepdims=True)
        span = pl.ds(frame * per_frame, per_frame)
        cond[span] = (q_ref[span].astype(F32) + offset).astype(BF)

    wait_bytes(wg.at[0, pl.ds(0, nx - 1), 0], small_recv.at[AGX])
    over_y(lambda y: small(wg.at[yy, :, core], wg.at[yy, :, core], AGY, at_y(y)))
    scatter_in(0, cond, qb, 0)
    wait_bytes(prev, small_recv.at[LAM])
    lam = lam_ref[...].astype(F32)
    before = jnp.where(me > 0, prev[...].astype(F32), 0.0)
    delta = jnp.concatenate(
        [lam[:per_frame] - before, lam[per_frame:] - lam[:per_frame]], axis=0
    ).astype(BF)
    wait_bytes(wg.at[pl.ds(0, ny - 1), :, 0], small_recv.at[AGY])
    small(wg.at[:, :, core], wg.at[:, :, core], AGC, other_core)
    scatter_in(2, v_ref, vb, 0)
    scatter_in(3, g_ref, gb, 0)
    delta_t = delta.T
    wait_bytes(wg.at[:, :, 0], small_recv.at[AGC])
    slab = lam_width // ny
    encoded = jnp.zeros((here, lam_width), F32)
    for y in range(ny):
        encoded += dot(delta[:, y * slab:(y + 1) * slab], wg[y].reshape(slab, lam_width))
    sig = jax.nn.sigmoid(encoded)
    act = encoded * sig
    slope = sig * (1.0 + encoded * (1.0 - sig))
    book = book_ref[...]
    book_ids = lax.broadcasted_iota(jnp.int32, book.shape, 0)
    term = jnp.zeros(book.shape, F32)
    graded = []
    for frame, code in ((0, code_a), (1, code_b)):
        span = slice(frame * per_frame, (frame + 1) * per_frame)
        pooled = jnp.sum(act[span], axis=0, keepdims=True) * (1.0 / per_frame)
        target = jnp.sum(jnp.where(book_ids == code, book, 0.0), axis=0, keepdims=True)
        frame_id = me * 2 + frame
        live = jnp.where((frame_id >= 1) & (frame_id != boundary), 1.0 / (2 * nt), 0.0)
        residual = (pooled - target) * live
        term -= jnp.where(book_ids == code, residual, 0.0)
        graded.append(residual * (1.0 / per_frame) * slope[span])
    encoded_grad = jnp.concatenate(graded, axis=0).astype(BF)
    for t in range(nt):
        cterm[t] = term[:, t * part:(t + 1) * part]
    cin[me] = cterm[me]
    over_t(lambda t: small(cterm.at[t], cin.at[me], CT, at_t(t)))
    for yx in range(ny * nx):
        lo = yx * nc * enc_rows
        piece = dot(delta_t[lo:lo + nc * enc_rows], encoded_grad).astype(BF)
        for c in range(nc):
            dw[c, yx // nx, yx % nx] = piece[c * enc_rows:(c + 1) * enc_rows]
    small(dw.at[nc - 1 - core], rc, RSC, other_core)

    def add_cores():
        wait_bytes(rc, small_recv.at[RSC])
        for y in range(ny):
            s1[y] = (dw[core, y].astype(F32) + rc[y].astype(F32)).astype(BF)
        over_y(lambda y: small(s1.at[y], ry.at[yy], RSY, at_y(y)))
        ry[yy] = s1[yy]

    def add_y():
        wait_bytes(ry.at[pl.ds(0, ny - 1)], small_recv.at[RSY])
        total = ry[0].astype(F32)
        for y in range(1, ny):
            total += ry[y].astype(F32)
        s2[...] = total.astype(BF)
        over_x(lambda x: small(s2.at[x], rx.at[xx], RSX, at_x(x)))
        rx[xx] = s2[xx]

    def add_x():
        wait_bytes(rx.at[pl.ds(0, nx - 1)], small_recv.at[RSX])
        total = rx[0].astype(F32)
        for x in range(1, nx):
            total += rx[x].astype(F32)
        total = total.astype(BF)
        for t in range(nt):
            s3[t] = total[:, t * part:(t + 1) * part]
        over_t(lambda t: small(s3.at[t], rt.at[me], RST, at_t(t)))
        rt[me] = s3[me]

    def add_t():
        wait_bytes(rt.at[pl.ds(0, nt - 1)], small_recv.at[RST])
        total = rt[0].astype(F32)
        for t in range(1, nt):
            total += rt[t].astype(F32)
        s4[...] = total.astype(BF)
        ge[:, lanes(me, part)] = s4[...]
        over_t(lambda t: small(s4, ge.at[:, lanes(me, part)], GE, at_t(t)))

    score_scale = 1.0 / math.sqrt(HS)
    exp_scale = score_scale * math.log2(math.e)

    def attend(head):
        for index, block in ((0, qb), (1, kb), (2, vb), (3, gb)):
            wait_bytes(block.at[head], in_recv.at[index, head])
        kt[...] = kb[head].T
        vt[...] = vb[head].T
        qt[...] = qb[head].T
        gt[...] = gb[head].T
        for c in reversed(range(rows // chunk)):
            size = (c + 1) * chunk
            span = slice(c * chunk, size)
            scores = dot(kb[head, :size], qt[:, span])
            frame_of = (lax.broadcasted_iota(jnp.int32, (1, chunk), 1) + c * chunk) // per_frame
            low = jnp.where(frame_of >= boundary, boundary, 0) * per_frame
            high = (frame_of + 1) * per_frame
            key_ids = lax.broadcasted_iota(jnp.int32, (size, chunk), 0)
            scores = jnp.where((key_ids >= low) & (key_ids < high), scores, NEG_FILL)
            top = jnp.max(scores, axis=0, keepdims=True)
            prob = jnp.exp2((scores - top) * exp_scale)
            prob = prob * (1.0 / jnp.sum(prob, axis=0, keepdims=True))
            weights = prob.astype(BF)
            out_t = dot(vt[:, :size], weights).astype(BF)
            ob[head, span] = out_t.T
            g_t = gt[:, span]
            grad_dot = jnp.sum(g_t.astype(F32) * out_t.astype(F32), axis=0, keepdims=True)
            prob_grad = dot(vb[head, :size], g_t)
            score_grad = (prob * ((prob_grad - grad_dot) * score_scale)).astype(BF)
            dqb[head, span] = dot(kt[:, :size], score_grad).astype(BF).T
            dk_part = dot(score_grad, qb[head, span])
            dv_part = dot(weights, gb[head, span])
            if size == rows:
                dk_acc[...] = dk_part
                dv_acc[...] = dv_part
            else:
                dk_acc[:size] += dk_part
                dv_acc[:size] += dv_part
        dkb[head] = dk_acc[...].astype(BF)
        dvb[head] = dv_acc[...].astype(BF)

    outputs = ((ob, o_out), (dqb, dq_out), (dkb, dk_out), (dvb, dv_out))

    def scatter_out(index, head):
        src, dst = outputs[index]
        columns = lanes(me * heads + head, HS)

        def block(t):
            return src.at[head, pl.ds(pl.multiple_of(t * here, here), here)]

        over_t(lambda t: send(
            block(t), dst.at[:, columns], out_send.at[index], out_recv.at[index], at_t(t)
        ))
        pltpu.make_async_copy(block(me), dst.at[:, columns], out_recv.at[index]).start()

    stages = [add_cores, add_y, add_x, add_t]
    inputs = ((k_ref, kb, 1), (cond, qb, 0), (v_ref, vb, 2), (g_ref, gb, 3))
    pieces = [(src, dst, index, head) for head in range(1, heads) for src, dst, index in inputs]

    def feed(count):
        for src, dst, index, head in pieces[:count]:
            scatter_in(index, src, dst, head)
        del pieces[:count]

    def advance():
        if stages:
            stages.pop(0)()

    feed(2)
    advance()
    feed(2)
    for head in range(heads):
        attend(head)
        if head < heads - 1:
            feed(1)
            advance()
            feed(1)
            scatter_out(0, head)
            scatter_out(1, head)
            feed(1)
            advance()
            feed(1)
            scatter_out(2, head)
            scatter_out(3, head)
    while stages:
        advance()

    wait_bytes(onehot.at[:, pl.ds(0, (nt - 1) * here)], small_recv.at[HOT])
    hot = onehot[...].astype(BF)
    for head in range(heads):
        blob[:, head * HS:(head + 1) * HS] = dot(hot, dqb[head])
    wait_bytes(cin.at[pl.ds(0, nt - 1)], small_recv.at[CT])
    total = cin[0]
    for t in range(1, nt):
        total += cin[t]
    blob[:, width:] = total
    small(blob, core_in, ARC, other_core)
    scatter_out(0, heads - 1)
    scatter_out(1, heads - 1)
    wait_bytes(core_in, small_recv.at[ARC])
    y_in[yy] = blob[...] + core_in[...]
    over_y(lambda y: small(y_in.at[yy], y_in.at[yy], ARY, at_y(y)))
    scatter_out(2, heads - 1)
    wait_bytes(y_in.at[pl.ds(0, ny - 1)], small_recv.at[ARY])
    total = y_in[0]
    for y in range(1, ny):
        total += y_in[y]
    x_in[xx] = total
    over_x(lambda x: small(x_in.at[xx], x_in.at[xx], ARX, at_x(x)))
    wait_bytes(x_in.at[pl.ds(0, nx - 1)], small_recv.at[ARX])
    total = x_in[0]
    for x in range(1, nx):
        total += x_in[x]
    wait_bytes(blob, small_send.at[ARC])
    blob[...] = total
    act_part, book_part = blob.at[:, pl.ds(0, width)], blob.at[:, pl.ds(width, part)]
    act_dst, book_dst = ga_out.at[:, lanes(me, width)], gc_out.at[:, lanes(me, part)]
    over_t(lambda t: small(act_part, act_dst, FA, at_t(t)))
    over_t(lambda t: small(book_part, book_dst, FC, at_t(t)))
    pltpu.make_async_copy(act_part, act_dst, small_recv.at[FA]).start()
    pltpu.make_async_copy(book_part, book_dst, small_recv.at[FC]).start()
    scatter_out(3, heads - 1)

    for index, dst in enumerate((o_out, dq_out, dk_out, dv_out)):
        wait_bytes(dst, out_recv.at[index])
    wait_bytes(ge.at[:, pl.ds(0, (nt - 1) * part)], small_recv.at[GE])
    store = pltpu.make_async_copy(ge, ge_out, load.at[0])
    store.start()
    store.wait()
    wait_bytes(ga_out, small_recv.at[FA])
    wait_bytes(gc_out, small_recv.at[FC])
    sent = qb.at[:, pl.ds(0, rows - here)]
    for index in range(4):
        wait_bytes(sent, in_send.at[index])
        wait_bytes(sent, out_send.at[index])
    for index, view in (
        (LAM, prev),
        (AGX, wg.at[0, pl.ds(0, nx - 1), 0]),
        (AGY, wg.at[pl.ds(0, ny - 1), :, 0]),
        (AGC, wg.at[:, :, 0]),
        (HOT, onehot.at[:, pl.ds(0, (nt - 1) * here)]),
        (RSC, rc),
        (RSY, ry.at[pl.ds(0, ny - 1)]),
        (RSX, rx.at[pl.ds(0, nx - 1)]),
        (RST, rt.at[pl.ds(0, nt - 1)]),
        (GE, ge.at[:, pl.ds(0, (nt - 1) * part)]),
        (CT, cin.at[pl.ds(0, nt - 1)]),
        (ARY, y_in.at[pl.ds(0, ny - 1)]),
        (ARX, x_in.at[pl.ds(0, nx - 1)]),
        (FA, ga_out.at[:, pl.ds(0, (nt - 1) * width)]),
        (FC, gc_out.at[:, pl.ds(0, (nt - 1) * part)]),
    ):
        wait_bytes(view, small_send.at[index])


def keep(*refs):
    raw, done = refs[:7], refs[7:14]
    held, sem_in, sem_out = refs[14:21], refs[21], refs[22]
    loads = [pltpu.make_async_copy(raw[i], held[i], sem_in.at[i]) for i in range(7)]
    for copy in loads:
        copy.start()
    stores = [
        pltpu.make_async_copy(held[i], done[i], sem_out.at[i]) for i in range(6)
    ]
    for i in range(6):
        loads[i].wait()
        stores[i].start()
    loads[6].wait()
    done[6][...] = held[6][...].astype(F32)
    for copy in stores:
        copy.wait()


def per_device(
    ny, nx, nc, nt, chunk,
    queries, keys, values, out_grad, action_table, lam_tokens, enc_weight, codebook,
    action_codes, episode_start,
):
    shape = queries.shape
    here = shape[1] * shape[2]
    wide = shape[3]
    lam_width = lam_tokens.shape[3]
    heads = wide // HS // nt
    rows = here * nt
    part = lam_width // nt
    enc_rows = enc_weight.shape[0]
    vmem = pl.BlockSpec(memory_space=pltpu.VMEM)
    smem = pl.BlockSpec(memory_space=pltpu.SMEM)
    anywhere = pl.BlockSpec(memory_space=pl.ANY)
    head_block = pltpu.VMEM((heads, rows, HS), BF)
    turned = pltpu.VMEM((HS, rows), BF)
    flops = heads * rows * rows * HS * 2 * 6 + 2 * 2 * here * lam_width * lam_width
    flat = jax.ShapeDtypeStruct((here, wide), BF)
    results = pl.pallas_call(
        functools.partial(kernel, (ny, nx, nc, nt, chunk)),
        out_shape=(
            flat, flat, flat, flat,
            jax.ShapeDtypeStruct(action_table.shape, F32),
            jax.ShapeDtypeStruct(codebook.shape, F32),
            jax.ShapeDtypeStruct(enc_weight.shape, BF),
        ),
        in_specs=[anywhere] * 8 + [smem, smem],
        out_specs=[anywhere] * 7,
        scratch_shapes=[
            pltpu.VMEM((here, wide), BF),
            pltpu.VMEM(action_table.shape, F32),
            pltpu.VMEM((here, lam_width), BF),
            pltpu.VMEM(codebook.shape, F32),
            pltpu.VMEM((here, wide), BF),
            head_block, head_block, head_block, head_block,
            head_block, head_block, head_block, head_block,
            turned, turned, turned, turned,
            pltpu.VMEM((rows, HS), F32),
            pltpu.VMEM((rows, HS), F32),
            pltpu.VMEM((NC, rows), F32),
            pltpu.VMEM((here // 2, lam_width), BF),
            pltpu.VMEM((ny, nx, nc, enc_rows, lam_width), BF),
            pltpu.VMEM((nc, ny, nx, enc_rows, lam_width), BF),
            pltpu.VMEM((ny, nx, enc_rows, lam_width), BF),
            pltpu.VMEM((ny, nx, enc_rows, lam_width), BF),
            pltpu.VMEM((ny, nx, enc_rows, lam_width), BF),
            pltpu.VMEM((nx, enc_rows, lam_width), BF),
            pltpu.VMEM((nx, enc_rows, lam_width), BF),
            pltpu.VMEM((nt, enc_rows, part), BF),
            pltpu.VMEM((nt, enc_rows, part), BF),
            pltpu.VMEM((enc_rows, part), BF),
            pltpu.VMEM((enc_rows, lam_width), BF),
            pltpu.VMEM((nt, NC, part), F32),
            pltpu.VMEM((nt, NC, part), F32),
            pltpu.VMEM((NC, heads * HS + part), F32),
            pltpu.VMEM((NC, heads * HS + part), F32),
            pltpu.VMEM((ny, NC, heads * HS + part), F32),
            pltpu.VMEM((nx, NC, heads * HS + part), F32),
            pltpu.SemaphoreType.DMA((5,)),
            pltpu.SemaphoreType.DMA((4, heads)),
            pltpu.SemaphoreType.DMA((4,)),
            pltpu.SemaphoreType.DMA((4,)),
            pltpu.SemaphoreType.DMA((4,)),
            pltpu.SemaphoreType.DMA((16,)),
            pltpu.SemaphoreType.DMA((16,)),
        ],
        compiler_params=pltpu.CompilerParams(
            collective_id=0, has_side_effects=True, vmem_limit_bytes=56 * 2**20
        ),
        cost_estimate=pl.CostEstimate(
            flops=flops, bytes_accessed=8 * here * wide * 2, transcendentals=heads * rows * rows
        ),
    )(
        queries.reshape(here, wide), keys.reshape(here, wide), values.reshape(here, wide),
        out_grad.reshape(here, wide), action_table, lam_tokens.reshape(here, lam_width),
        enc_weight, codebook, action_codes, episode_start,
    )
    results = pl.pallas_call(
        keep,
        out_shape=tuple(jax.ShapeDtypeStruct(r.shape, r.dtype) for r in results[:6])
        + (jax.ShapeDtypeStruct(enc_weight.shape, F32),),
        in_specs=[anywhere] * 7,
        out_specs=[anywhere] * 6 + [vmem],
        scratch_shapes=[pltpu.VMEM(r.shape, r.dtype) for r in results]
        + [pltpu.SemaphoreType.DMA((7,)), pltpu.SemaphoreType.DMA((6,))],
    )(*results)
    return tuple(r.reshape(shape) for r in results[:4]) + tuple(results[4:])


def solution(mesh, dims=(4, 4, 2), chunk=256):
    ny, nx, nc = dims
    nt = mesh.shape["tm"]
    frames = P("dp", "tm", None, None)
    return jax.shard_map(
        functools.partial(per_device, ny, nx, nc, nt, chunk),
        mesh=mesh,
        in_specs=(
            frames, frames, frames, frames, P(), frames, P("dp", None), P(), P("dp", "tm"), P("dp"),
        ),
        out_specs=(frames, frames, frames, frames, P(), P(), P("dp", None)),
        check_vma=False,
    )
```

```python
import functools
import math

import jax
import jax.numpy as jnp
from jax import lax
from jax.experimental import pallas as pl
from jax.experimental.pallas import tpu as pltpu
from jax.sharding import PartitionSpec as P

HS = 128
NC = 8
NEG_FILL = -1e30
ORDER = "iciyiidiieiisiiAoosiioosAoosooAtoototto"
MESH = pl.DeviceIdType.MESH
BF = jnp.bfloat16
F32 = jnp.float32


def dot(a, b):
    return jnp.dot(a, b, preferred_element_type=F32)


def wait_bytes(view, sem):
    pltpu.make_async_copy(view, view, sem).wait()


def kernel(
    sizes,
    q_hbm, k_ref, v_ref, g_ref, tab_hbm, lam_hbm, enc_hbm, book_hbm, code_ref, start_ref,
    o_out, dq_out, dk_out, dv_out, ga_out, gc_out, ge_out,
    q_ref, tab_ref, lam_ref, book_ref, cond, qb, kb, vb, gb, ob, dqb, dkb, dvb, kt, vt, qt, gt, dk_acc, dv_acc,
    codes, prev, wg, dw, rc, s1, ry, s2, rx, s3, rt, s4, ge,
    cterm, cin, blob, core_in, y_in, x_in, sums, ga, gc,
    load, in_recv, in_send, out_recv, out_send, small_recv, small_send,
):
    ny, nx, nc, nt, chunk = sizes
    heads = qb.shape[0]
    rows = qb.shape[1]
    here = rows // nt
    per_frame = here // 2
    width = heads * HS
    lam_width = lam_ref.shape[1]
    part = lam_width // nt
    enc_rows = enc_hbm.shape[0]
    dp = lax.axis_index("dp")
    me = lax.axis_index("tm")
    core = dp % nc
    xx = (dp // nc) % nx
    yy = dp // (nc * nx)

    def at_t(t):
        return (dp, t)

    def at_x(x):
        return ((yy * nx + x) * nc + core, me)

    def at_y(y):
        return ((y * nx + xx) * nc + core, me)

    other_core = ((yy * nx + xx) * nc + (nc - 1 - core), me)

    def over_t(fn):
        def body(i, carry):
            step = nt // 2 + (1 - 2 * (i % 2)) * ((i + 1) // 2)
            fn((me + step) % nt)
            return carry

        lax.fori_loop(0, nt - 1, body, 0)

    def over_x(fn):
        def body(i, carry):
            fn((xx + 1 + i) % nx)
            return carry

        lax.fori_loop(0, nx - 1, body, 0)

    def over_y(fn):
        def body(i, carry):
            fn((yy + 1 + i) % ny)
            return carry

        lax.fori_loop(0, ny - 1, body, 0)

    own_rows = wg.at[yy, xx, core]
    loads = [
        pltpu.make_async_copy(src, dst, load.at[i])
        for i, (src, dst) in enumerate((
            (enc_hbm, own_rows), (lam_hbm, lam_ref), (q_hbm, q_ref),
            (tab_hbm, tab_ref), (book_hbm, book_ref),
        ))
    ]
    for copy in loads:
        copy.start()

    barrier = pltpu.get_barrier_semaphore()

    def greet(device):
        pl.semaphore_signal(barrier, inc=1, device_id=device, device_id_type=MESH)

    over_t(lambda t: greet(at_t(t)))
    over_x(lambda x: greet(at_x(x)))
    over_y(lambda y: greet(at_y(y)))
    greet(other_core)
    pl.semaphore_wait(barrier, (nt - 1) + (nx - 1) + (ny - 1) + 1)

    def send(src, dst, sem_s, sem_r, device):
        pltpu.make_async_remote_copy(
            src_ref=src, dst_ref=dst, send_sem=sem_s, recv_sem=sem_r,
            device_id=device, device_id_type=MESH,
        ).start()

    LAM, AGX, AGY, AGC, HOT, RSC, RSY, RSX, RST, GE, CT, ARC, ARY, ARX, FA = range(15)

    def small(src, dst, index, device):
        send(src, dst, small_send.at[index], small_recv.at[index], device)

    def lanes(index, size):
        return pl.ds(pl.multiple_of(index * size, size), size)

    loads[0].wait()
    over_x(lambda x: small(own_rows, own_rows, AGX, at_x(x)))
    loads[1].wait()
    small(lam_ref.at[pl.ds(per_frame, per_frame)], prev, LAM, at_t((me + 1) % nt))
    code_a, code_b = code_ref[0, 0], code_ref[0, 1]
    boundary = start_ref[0]
    lane_code = jnp.where(
        lax.broadcasted_iota(jnp.int32, (1, here), 1) < per_frame, code_a, code_b
    )
    codes[me] = lane_code.astype(F32)
    over_t(lambda t: small(codes.at[me], codes.at[me], HOT, at_t(t)))

    mine = pl.ds(pl.multiple_of(me * here, here), here)

    def scatter_in(index, src, dst, head):
        def one(t):
            send(
                src.at[:, lanes(t * heads + head, HS)], dst.at[head, mine],
                in_send.at[index], in_recv.at[index, head], at_t(t),
            )

        over_t(one)
        pltpu.make_async_copy(
            src.at[:, lanes(me * heads + head, HS)], dst.at[head, mine], in_recv.at[index, head]
        ).start()

    def condition():
        for copy in loads[2:]:
            copy.wait()
        table = tab_ref[...]
        code_ids = lax.broadcasted_iota(jnp.int32, table.shape, 0)
        for frame, code in ((0, code_a), (1, code_b)):
            offset = jnp.sum(jnp.where(code_ids == code, table, 0.0), axis=0, keepdims=True)
            span = pl.ds(frame * per_frame, per_frame)
            cond[span] = (q_ref[span].astype(F32) + offset).astype(BF)

    def rows_over_y():
        wait_bytes(wg.at[0, pl.ds(0, nx - 1), 0], small_recv.at[AGX])
        over_y(lambda y: small(wg.at[yy, :, core], wg.at[yy, :, core], AGY, at_y(y)))

    def rows_over_cores():
        wait_bytes(prev, small_recv.at[LAM])
        lam = lam_ref[...].astype(F32)
        before = jnp.where(me > 0, prev[...].astype(F32), 0.0)
        delta = jnp.concatenate(
            [lam[:per_frame] - before, lam[per_frame:] - lam[:per_frame]], axis=0
        ).astype(BF)
        wait_bytes(wg.at[pl.ds(0, ny - 1), :, 0], small_recv.at[AGY])
        small(wg.at[:, :, core], wg.at[:, :, core], AGC, other_core)
        return delta

    def encode(delta):
        delta_t = delta.T
        wait_bytes(wg.at[:, :, 0], small_recv.at[AGC])
        slab = lam_width // ny
        encoded = jnp.zeros((here, lam_width), F32)
        for y in range(ny):
            encoded += dot(delta[:, y * slab:(y + 1) * slab], wg[y].reshape(slab, lam_width))
        sig = jax.nn.sigmoid(encoded)
        act = encoded * sig
        slope = sig * (1.0 + encoded * (1.0 - sig))
        book = book_ref[...]
        book_ids = lax.broadcasted_iota(jnp.int32, book.shape, 0)
        term = jnp.zeros(book.shape, F32)
        graded = []
        for frame, code in ((0, code_a), (1, code_b)):
            span = slice(frame * per_frame, (frame + 1) * per_frame)
            pooled = jnp.sum(act[span], axis=0, keepdims=True) * (1.0 / per_frame)
            target = jnp.sum(jnp.where(book_ids == code, book, 0.0), axis=0, keepdims=True)
            frame_id = me * 2 + frame
            live = jnp.where((frame_id >= 1) & (frame_id != boundary), 1.0 / (2 * nt), 0.0)
            residual = (pooled - target) * live
            term -= jnp.where(book_ids == code, residual, 0.0)
            graded.append(residual * (1.0 / per_frame) * slope[span])
        encoded_grad = jnp.concatenate(graded, axis=0).astype(BF)
        for t in range(nt):
            cterm[t] = term[:, t * part:(t + 1) * part]
        cin[me] = cterm[me]
        over_t(lambda t: small(cterm.at[t], cin.at[me], CT, at_t(t)))
        for yx in range(ny * nx):
            lo = yx * nc * enc_rows
            piece = dot(delta_t[lo:lo + nc * enc_rows], encoded_grad).astype(BF)
            for c in range(nc):
                dw[c, yx // nx, yx % nx] = piece[c * enc_rows:(c + 1) * enc_rows]
        small(dw.at[nc - 1 - core], rc, RSC, other_core)

    def add_cores():
        wait_bytes(rc, small_recv.at[RSC])
        for y in range(ny):
            s1[y] = (dw[core, y].astype(F32) + rc[y].astype(F32)).astype(BF)
        over_y(lambda y: small(s1.at[y], ry.at[yy], RSY, at_y(y)))
        ry[yy] = s1[yy]

    def add_y():
        wait_bytes(ry.at[pl.ds(0, ny - 1)], small_recv.at[RSY])
        total = ry[0].astype(F32)
        for y in range(1, ny):
            total += ry[y].astype(F32)
        s2[...] = total.astype(BF)
        over_x(lambda x: small(s2.at[x], rx.at[xx], RSX, at_x(x)))
        rx[xx] = s2[xx]

    def add_x():
        wait_bytes(rx.at[pl.ds(0, nx - 1)], small_recv.at[RSX])
        total = rx[0].astype(F32)
        for x in range(1, nx):
            total += rx[x].astype(F32)
        total = total.astype(BF)
        for t in range(nt):
            s3[t] = total[:, t * part:(t + 1) * part]
        over_t(lambda t: small(s3.at[t], rt.at[me], RST, at_t(t)))
        rt[me] = s3[me]

    def add_t():
        wait_bytes(rt.at[pl.ds(0, nt - 1)], small_recv.at[RST])
        total = rt[0].astype(F32)
        for t in range(1, nt):
            total += rt[t].astype(F32)
        s4[...] = total.astype(BF)
        ge[:, lanes(me, part)] = s4[...]
        over_t(lambda t: small(s4, ge.at[:, lanes(me, part)], GE, at_t(t)))

    score_scale = 1.0 / math.sqrt(HS)
    exp_scale = score_scale * math.log2(math.e)

    def attend(head):
        for index, block in ((0, qb), (1, kb), (2, vb), (3, gb)):
            wait_bytes(block.at[head], in_recv.at[index, head])
        kt[...] = kb[head].T
        vt[...] = vb[head].T
        qt[...] = qb[head].T
        gt[...] = gb[head].T
        for c in reversed(range(rows // chunk)):
            size = (c + 1) * chunk
            span = slice(c * chunk, size)
            scores = dot(kb[head, :size], qt[:, span])
            frame_of = (lax.broadcasted_iota(jnp.int32, (1, chunk), 1) + c * chunk) // per_frame
            low = jnp.where(frame_of >= boundary, boundary, 0) * per_frame
            high = (frame_of + 1) * per_frame
            key_ids = lax.broadcasted_iota(jnp.int32, (size, chunk), 0)
            scores = jnp.where((key_ids >= low) & (key_ids < high), scores, NEG_FILL)
            top = jnp.max(scores, axis=0, keepdims=True)
            prob = jnp.exp2((scores - top) * exp_scale)
            prob = prob * (1.0 / jnp.sum(prob, axis=0, keepdims=True))
            weights = prob.astype(BF)
            out_t = dot(vt[:, :size], weights).astype(BF)
            ob[head, span] = out_t.T
            g_t = gt[:, span]
            grad_dot = jnp.sum(g_t.astype(F32) * out_t.astype(F32), axis=0, keepdims=True)
            prob_grad = dot(vb[head, :size], g_t)
            score_grad = (prob * ((prob_grad - grad_dot) * score_scale)).astype(BF)
            dqb[head, span] = dot(kt[:, :size], score_grad).astype(BF).T
            dk_part = dot(score_grad, qb[head, span])
            dv_part = dot(weights, gb[head, span])
            if size == rows:
                dk_acc[...] = dk_part
                dv_acc[...] = dv_part
            else:
                dk_acc[:size] += dk_part
                dv_acc[:size] += dv_part
        dkb[head] = dk_acc[...].astype(BF)
        dvb[head] = dv_acc[...].astype(BF)

    outputs = ((ob, o_out), (dqb, dq_out), (dkb, dk_out), (dvb, dv_out))

    def scatter_out(index, head):
        src, dst = outputs[index]
        columns = lanes(me * heads + head, HS)

        def block(t):
            return src.at[head, pl.ds(pl.multiple_of(t * here, here), here)]

        over_t(lambda t: send(
            block(t), dst.at[:, columns], out_send.at[index], out_recv.at[index], at_t(t)
        ))
        pltpu.make_async_copy(block(me), dst.at[:, columns], out_recv.at[index]).start()

    def sum_over_cores():
        wait_bytes(codes.at[pl.ds(0, nt - 1)], small_recv.at[HOT])
        all_codes = jnp.concatenate([codes[t] for t in range(nt)], axis=1)
        code_rows = lax.broadcasted_iota(jnp.int32, (NC, rows), 0).astype(F32)
        hot = (code_rows == all_codes).astype(BF)
        for head in range(heads):
            blob[:, head * HS:(head + 1) * HS] = dot(hot, dqb[head])
        wait_bytes(cin.at[pl.ds(0, nt - 1)], small_recv.at[CT])
        total = cin[0]
        for t in range(1, nt):
            total += cin[t]
        blob[:, width:] = total
        small(blob, core_in, ARC, other_core)

    def sum_over_y():
        wait_bytes(core_in, small_recv.at[ARC])
        y_in[yy] = blob[...] + core_in[...]
        over_y(lambda y: small(y_in.at[yy], y_in.at[yy], ARY, at_y(y)))

    def sum_over_x():
        wait_bytes(y_in.at[pl.ds(0, ny - 1)], small_recv.at[ARY])
        total = y_in[0]
        for y in range(1, ny):
            total += y_in[y]
        x_in[xx] = total
        over_x(lambda x: small(x_in.at[xx], x_in.at[xx], ARX, at_x(x)))

    def share_sums():
        wait_bytes(x_in.at[pl.ds(0, nx - 1)], small_recv.at[ARX])
        total = x_in[0]
        for x in range(1, nx):
            total += x_in[x]
        half = (width + part) // 2
        sums[me] = jnp.concatenate([total[:, :half], total[:, half:]], axis=0).astype(BF)
        over_t(lambda t: small(sums.at[me], sums.at[me], FA, at_t(t)))

    inputs = ((k_ref, kb, 1), (cond, qb, 0), (v_ref, vb, 2), (g_ref, gb, 3))
    pieces = [(index, src, dst, head) for head in range(heads) for src, dst, index in inputs]
    results = [(index, head) for head in range(heads) for index in range(4)]
    steps = {
        "c": [condition], "y": [rows_over_y], "d": [rows_over_cores],
        "s": [add_cores, add_y, add_x, add_t],
        "t": [sum_over_cores, sum_over_y, sum_over_x, share_sums],
    }
    done = 0
    for step in ORDER:
        if step == "i":
            if pieces:
                scatter_in(*pieces.pop(0))
        elif step == "o":
            if results:
                scatter_out(*results.pop(0))
        elif step == "A":
            if done < heads:
                attend(done)
            done += 1
        elif step == "d":
            delta = rows_over_cores()
        elif step == "e":
            encode(delta)
        else:
            steps[step].pop(0)()

    for index, dst in enumerate((o_out, dq_out, dk_out, dv_out)):
        wait_bytes(dst, out_recv.at[index])
    wait_bytes(ge.at[:, pl.ds(0, (nt - 1) * part)], small_recv.at[GE])
    wait_bytes(sums.at[pl.ds(0, nt - 1)], small_recv.at[FA])
    for t in range(nt):
        got = sums[t].astype(F32)
        got = jnp.concatenate([got[:NC], got[NC:]], axis=1)
        ga[:, t * width:(t + 1) * width] = got[:, :width]
        gc[:, t * part:(t + 1) * part] = got[:, width:]
    ends = [
        pltpu.make_async_copy(src, dst, load.at[i])
        for i, (src, dst) in enumerate(((ge, ge_out), (ga, ga_out), (gc, gc_out)))
    ]
    for copy in ends:
        copy.start()
    for copy in ends:
        copy.wait()
    sent = qb.at[:, pl.ds(0, rows - here)]
    for index in range(4):
        wait_bytes(sent, in_send.at[index])
        wait_bytes(sent, out_send.at[index])
    for index, view in (
        (LAM, prev),
        (AGX, wg.at[0, pl.ds(0, nx - 1), 0]),
        (AGY, wg.at[pl.ds(0, ny - 1), :, 0]),
        (AGC, wg.at[:, :, 0]),
        (HOT, codes.at[pl.ds(0, nt - 1)]),
        (RSC, rc),
        (ARC, core_in),
        (RSY, ry.at[pl.ds(0, ny - 1)]),
        (RSX, rx.at[pl.ds(0, nx - 1)]),
        (RST, rt.at[pl.ds(0, nt - 1)]),
        (GE, ge.at[:, pl.ds(0, (nt - 1) * part)]),
        (CT, cin.at[pl.ds(0, nt - 1)]),
        (ARY, y_in.at[pl.ds(0, ny - 1)]),
        (ARX, x_in.at[pl.ds(0, nx - 1)]),
        (FA, sums.at[pl.ds(0, nt - 1)]),
    ):
        wait_bytes(view, small_send.at[index])


def keep(pieces, *refs):
    raw, done = refs[:7], refs[7:14]
    held, sem_in, sem_out = refs[14:21], refs[21], refs[22]
    loads, stores = [], []
    for piece in range(pieces):
        for i in range(7):
            whole = raw[i].shape[0]
            rows = whole // pieces if i < 4 else whole
            if i >= 4 and piece:
                continue
            span = pl.ds(piece * rows, rows)
            loads.append(pltpu.make_async_copy(
                raw[i].at[span], held[i].at[span], sem_in.at[i, piece]))
            if i < 6:
                stores.append(pltpu.make_async_copy(
                    held[i].at[span], done[i].at[span], sem_out.at[i, piece]))
            else:
                stores.append(None)
    for load in loads:
        load.start()
    for load, store in zip(loads, stores):
        load.wait()
        if store is None:
            done[6][...] = held[6][...].astype(F32)
        else:
            store.start()
    for store in stores:
        if store is not None:
            store.wait()


def per_device(
    ny, nx, nc, nt, chunk,
    queries, keys, values, out_grad, action_table, lam_tokens, enc_weight, codebook,
    action_codes, episode_start,
):
    shape = queries.shape
    here = shape[1] * shape[2]
    wide = shape[3]
    lam_width = lam_tokens.shape[3]
    heads = wide // HS // nt
    rows = here * nt
    part = lam_width // nt
    enc_rows = enc_weight.shape[0]
    vmem = pl.BlockSpec(memory_space=pltpu.VMEM)
    smem = pl.BlockSpec(memory_space=pltpu.SMEM)
    anywhere = pl.BlockSpec(memory_space=pl.ANY)
    head_block = pltpu.VMEM((heads, rows, HS), BF)
    turned = pltpu.VMEM((HS, rows), BF)
    flops = heads * rows * rows * HS * 2 * 6 + 2 * 2 * here * lam_width * lam_width
    flat = jax.ShapeDtypeStruct((here, wide), BF)
    results = pl.pallas_call(
        functools.partial(kernel, (ny, nx, nc, nt, chunk)),
        out_shape=(
            flat, flat, flat, flat,
            jax.ShapeDtypeStruct(action_table.shape, F32),
            jax.ShapeDtypeStruct(codebook.shape, F32),
            jax.ShapeDtypeStruct(enc_weight.shape, BF),
        ),
        in_specs=[anywhere] * 8 + [smem, smem],
        out_specs=[anywhere] * 7,
        scratch_shapes=[
            pltpu.VMEM((here, wide), BF),
            pltpu.VMEM(action_table.shape, F32),
            pltpu.VMEM((here, lam_width), BF),
            pltpu.VMEM(codebook.shape, F32),
            pltpu.VMEM((here, wide), BF),
            head_block, head_block, head_block, head_block,
            head_block, head_block, head_block, head_block,
            turned, turned, turned, turned,
            pltpu.VMEM((rows, HS), F32),
            pltpu.VMEM((rows, HS), F32),
            pltpu.VMEM((nt, 1, here), F32),
            pltpu.VMEM((here // 2, lam_width), BF),
            pltpu.VMEM((ny, nx, nc, enc_rows, lam_width), BF),
            pltpu.VMEM((nc, ny, nx, enc_rows, lam_width), BF),
            pltpu.VMEM((ny, nx, enc_rows, lam_width), BF),
            pltpu.VMEM((ny, nx, enc_rows, lam_width), BF),
            pltpu.VMEM((ny, nx, enc_rows, lam_width), BF),
            pltpu.VMEM((nx, enc_rows, lam_width), BF),
            pltpu.VMEM((nx, enc_rows, lam_width), BF),
            pltpu.VMEM((nt, enc_rows, part), BF),
            pltpu.VMEM((nt, enc_rows, part), BF),
            pltpu.VMEM((enc_rows, part), BF),
            pltpu.VMEM((enc_rows, lam_width), BF),
            pltpu.VMEM((nt, NC, part), F32),
            pltpu.VMEM((nt, NC, part), F32),
            pltpu.VMEM((NC, heads * HS + part), F32),
            pltpu.VMEM((NC, heads * HS + part), F32),
            pltpu.VMEM((ny, NC, heads * HS + part), F32),
            pltpu.VMEM((nx, NC, heads * HS + part), F32),
            pltpu.VMEM((nt, 2 * NC, (heads * HS + part) // 2), BF),
            pltpu.VMEM(action_table.shape, F32),
            pltpu.VMEM(codebook.shape, F32),
            pltpu.SemaphoreType.DMA((5,)),
            pltpu.SemaphoreType.DMA((4, heads)),
            pltpu.SemaphoreType.DMA((4,)),
            pltpu.SemaphoreType.DMA((4,)),
            pltpu.SemaphoreType.DMA((4,)),
            pltpu.SemaphoreType.DMA((16,)),
            pltpu.SemaphoreType.DMA((16,)),
        ],
        compiler_params=pltpu.CompilerParams(
            collective_id=0, has_side_effects=True, vmem_limit_bytes=56 * 2**20
        ),
        cost_estimate=pl.CostEstimate(
            flops=flops, bytes_accessed=8 * here * wide * 2, transcendentals=heads * rows * rows
        ),
    )(
        queries.reshape(here, wide), keys.reshape(here, wide), values.reshape(here, wide),
        out_grad.reshape(here, wide), action_table, lam_tokens.reshape(here, lam_width),
        enc_weight, codebook, action_codes, episode_start,
    )
    results = pl.pallas_call(
        functools.partial(keep, 1),
        out_shape=tuple(jax.ShapeDtypeStruct(r.shape, r.dtype) for r in results[:6])
        + (jax.ShapeDtypeStruct(enc_weight.shape, F32),),
        in_specs=[anywhere] * 7,
        out_specs=[anywhere] * 6 + [vmem],
        scratch_shapes=[pltpu.VMEM(r.shape, r.dtype) for r in results]
        + [pltpu.SemaphoreType.DMA((7, 1)), pltpu.SemaphoreType.DMA((6, 1))],
    )(*results)
    return tuple(r.reshape(shape) for r in results[:4]) + tuple(results[4:])


def solution(mesh, dims=(4, 4, 2), chunk=256):
    ny, nx, nc = dims
    nt = mesh.shape["tm"]
    frames = P("dp", "tm", None, None)
    return jax.shard_map(
        functools.partial(per_device, ny, nx, nc, nt, chunk),
        mesh=mesh,
        in_specs=(
            frames, frames, frames, frames, P(), frames, P("dp", None), P(), P("dp", "tm"), P("dp"),
        ),
        out_specs=(frames, frames, frames, frames, P(), P(), P("dp", None)),
        check_vma=False,
    )
```

```python
import functools
import math

import jax
import jax.numpy as jnp
from jax import lax
from jax.experimental import pallas as pl
from jax.experimental.pallas import tpu as pltpu
from jax.sharding import PartitionSpec as P

HS = 128
NC = 8
NEG_FILL = -1e30
ORDER = "iciyiidiieiisiiAoosiioosAoosooAtoototto"
MESH = pl.DeviceIdType.MESH
BF = jnp.bfloat16
F32 = jnp.float32


def dot(a, b):
    return jnp.dot(a, b, preferred_element_type=F32)


def wait_bytes(view, sem):
    pltpu.make_async_copy(view, view, sem).wait()


def kernel(
    sizes,
    q_hbm, k_ref, v_ref, g_ref, tab_hbm, lam_hbm, enc_hbm, book_hbm, code_ref, start_ref,
    o_out, dq_out, dk_out, dv_out, ga_out, gc_out, ge_out,
    q_ref, tab_ref, lam_ref, book_ref, cond, qb, kb, vb, gb, ob, dqb, dkb, dvb, kt, vt, qt, gt, dk_acc, dv_acc,
    codes, prev, wg, dw, rc, s1, ry, s2, rx, s3, rt, s4, ge,
    cterm, cin, blob, core_in, y_in, x_in, sums, ga, gc,
    load, in_recv, in_send, out_recv, out_send, small_recv, small_send,
):
    ny, nx, nc, nt, chunk = sizes
    heads = qb.shape[0]
    rows = qb.shape[1]
    here = rows // nt
    per_frame = here // 2
    width = heads * HS
    lam_width = lam_ref.shape[1]
    part = lam_width // nt
    enc_rows = enc_hbm.shape[0]
    dp = lax.axis_index("dp")
    me = lax.axis_index("tm")
    core = dp % nc
    xx = (dp // nc) % nx
    yy = dp // (nc * nx)

    def at_t(t):
        return (dp, t)

    def at_x(x):
        return ((yy * nx + x) * nc + core, me)

    def at_y(y):
        return ((y * nx + xx) * nc + core, me)

    other_core = ((yy * nx + xx) * nc + (nc - 1 - core), me)

    def over_t(fn):
        def body(i, carry):
            step = nt // 2 + (1 - 2 * (i % 2)) * ((i + 1) // 2)
            fn((me + step) % nt)
            return carry

        lax.fori_loop(0, nt - 1, body, 0)

    def over_x(fn):
        def body(i, carry):
            fn((xx + 1 + i) % nx)
            return carry

        lax.fori_loop(0, nx - 1, body, 0)

    def over_y(fn):
        def body(i, carry):
            fn((yy + 1 + i) % ny)
            return carry

        lax.fori_loop(0, ny - 1, body, 0)

    own_rows = wg.at[yy, xx, core]
    loads = [
        pltpu.make_async_copy(src, dst, load.at[i])
        for i, (src, dst) in enumerate((
            (enc_hbm, own_rows), (lam_hbm, lam_ref), (q_hbm, q_ref),
            (tab_hbm, tab_ref), (book_hbm, book_ref),
        ))
    ]
    for copy in loads:
        copy.start()

    barrier = pltpu.get_barrier_semaphore()

    def greet(device):
        pl.semaphore_signal(barrier, inc=1, device_id=device, device_id_type=MESH)

    over_t(lambda t: greet(at_t(t)))
    over_x(lambda x: greet(at_x(x)))
    over_y(lambda y: greet(at_y(y)))
    greet(other_core)
    pl.semaphore_wait(barrier, (nt - 1) + (nx - 1) + (ny - 1) + 1)

    def send(src, dst, sem_s, sem_r, device):
        pltpu.make_async_remote_copy(
            src_ref=src, dst_ref=dst, send_sem=sem_s, recv_sem=sem_r,
            device_id=device, device_id_type=MESH,
        ).start()

    LAM, AGX, AGY, AGC, HOT, RSC, RSY, RSX, RST, GE, CT, ARC, ARY, ARX, FA = range(15)

    def small(src, dst, index, device):
        send(src, dst, small_send.at[index], small_recv.at[index], device)

    def lanes(index, size):
        return pl.ds(pl.multiple_of(index * size, size), size)

    loads[0].wait()
    over_x(lambda x: small(own_rows, own_rows, AGX, at_x(x)))
    loads[1].wait()
    small(lam_ref.at[pl.ds(per_frame, per_frame)], prev, LAM, at_t((me + 1) % nt))
    code_a, code_b = code_ref[0, 0], code_ref[0, 1]
    boundary = start_ref[0]
    lane_code = jnp.where(
        lax.broadcasted_iota(jnp.int32, (1, here), 1) < per_frame, code_a, code_b
    )
    codes[me] = lane_code.astype(F32)
    over_t(lambda t: small(codes.at[me], codes.at[me], HOT, at_t(t)))

    mine = pl.ds(pl.multiple_of(me * here, here), here)

    def scatter_in(index, src, dst, head):
        def one(t):
            send(
                src.at[:, lanes(t * heads + head, HS)], dst.at[head, mine],
                in_send.at[index], in_recv.at[index, head], at_t(t),
            )

        over_t(one)
        pltpu.make_async_copy(
            src.at[:, lanes(me * heads + head, HS)], dst.at[head, mine], in_recv.at[index, head]
        ).start()

    def condition():
        for copy in loads[2:]:
            copy.wait()
        table = tab_ref[...]
        code_ids = lax.broadcasted_iota(jnp.int32, table.shape, 0)
        for frame, code in ((0, code_a), (1, code_b)):
            offset = jnp.sum(jnp.where(code_ids == code, table, 0.0), axis=0, keepdims=True)
            span = pl.ds(frame * per_frame, per_frame)
            cond[span] = (q_ref[span].astype(F32) + offset).astype(BF)

    def rows_over_y():
        wait_bytes(wg.at[0, pl.ds(0, nx - 1), 0], small_recv.at[AGX])
        over_y(lambda y: small(wg.at[yy, :, core], wg.at[yy, :, core], AGY, at_y(y)))

    def rows_over_cores():
        wait_bytes(prev, small_recv.at[LAM])
        lam = lam_ref[...].astype(F32)
        before = jnp.where(me > 0, prev[...].astype(F32), 0.0)
        delta = jnp.concatenate(
            [lam[:per_frame] - before, lam[per_frame:] - lam[:per_frame]], axis=0
        ).astype(BF)
        wait_bytes(wg.at[pl.ds(0, ny - 1), :, 0], small_recv.at[AGY])
        small(wg.at[:, :, core], wg.at[:, :, core], AGC, other_core)
        return delta

    def encode(delta):
        delta_t = delta.T
        wait_bytes(wg.at[:, :, 0], small_recv.at[AGC])
        slab = lam_width // ny
        encoded = jnp.zeros((here, lam_width), F32)
        for y in range(ny):
            encoded += dot(delta[:, y * slab:(y + 1) * slab], wg[y].reshape(slab, lam_width))
        sig = jax.nn.sigmoid(encoded)
        act = encoded * sig
        slope = sig * (1.0 + encoded * (1.0 - sig))
        book = book_ref[...]
        book_ids = lax.broadcasted_iota(jnp.int32, book.shape, 0)
        term = jnp.zeros(book.shape, F32)
        graded = []
        for frame, code in ((0, code_a), (1, code_b)):
            span = slice(frame * per_frame, (frame + 1) * per_frame)
            pooled = jnp.sum(act[span], axis=0, keepdims=True) * (1.0 / per_frame)
            target = jnp.sum(jnp.where(book_ids == code, book, 0.0), axis=0, keepdims=True)
            frame_id = me * 2 + frame
            live = jnp.where((frame_id >= 1) & (frame_id != boundary), 1.0 / (2 * nt), 0.0)
            residual = (pooled - target) * live
            term -= jnp.where(book_ids == code, residual, 0.0)
            graded.append(residual * (1.0 / per_frame) * slope[span])
        encoded_grad = jnp.concatenate(graded, axis=0).astype(BF)
        for t in range(nt):
            cterm[t] = term[:, t * part:(t + 1) * part]
        cin[me] = cterm[me]
        over_t(lambda t: small(cterm.at[t], cin.at[me], CT, at_t(t)))
        for yx in range(ny * nx):
            lo = yx * nc * enc_rows
            piece = dot(delta_t[lo:lo + nc * enc_rows], encoded_grad).astype(BF)
            for c in range(nc):
                dw[c, yx // nx, yx % nx] = piece[c * enc_rows:(c + 1) * enc_rows]
        small(dw.at[nc - 1 - core], rc, RSC, other_core)

    def add_cores():
        wait_bytes(rc, small_recv.at[RSC])
        for y in range(ny):
            s1[y] = (dw[core, y].astype(F32) + rc[y].astype(F32)).astype(BF)
        over_y(lambda y: small(s1.at[y], ry.at[yy], RSY, at_y(y)))
        ry[yy] = s1[yy]

    def add_y():
        wait_bytes(ry.at[pl.ds(0, ny - 1)], small_recv.at[RSY])
        total = ry[0].astype(F32)
        for y in range(1, ny):
            total += ry[y].astype(F32)
        s2[...] = total.astype(BF)
        over_x(lambda x: small(s2.at[x], rx.at[xx], RSX, at_x(x)))
        rx[xx] = s2[xx]

    def add_x():
        wait_bytes(rx.at[pl.ds(0, nx - 1)], small_recv.at[RSX])
        total = rx[0].astype(F32)
        for x in range(1, nx):
            total += rx[x].astype(F32)
        total = total.astype(BF)
        for t in range(nt):
            s3[t] = total[:, t * part:(t + 1) * part]
        over_t(lambda t: small(s3.at[t], rt.at[me], RST, at_t(t)))
        rt[me] = s3[me]

    def add_t():
        wait_bytes(rt.at[pl.ds(0, nt - 1)], small_recv.at[RST])
        total = rt[0].astype(F32)
        for t in range(1, nt):
            total += rt[t].astype(F32)
        s4[...] = total.astype(BF)
        ge[:, lanes(me, part)] = s4[...]
        over_t(lambda t: small(s4, ge.at[:, lanes(me, part)], GE, at_t(t)))

    score_scale = 1.0 / math.sqrt(HS)
    exp_scale = score_scale * math.log2(math.e)

    def attend(head):
        for index, block in ((0, qb), (1, kb), (2, vb), (3, gb)):
            wait_bytes(block.at[head], in_recv.at[index, head])
        kt[...] = kb[head].T
        vt[...] = vb[head].T
        qt[...] = qb[head].T
        gt[...] = gb[head].T
        for c in reversed(range(rows // chunk)):
            size = (c + 1) * chunk
            span = slice(c * chunk, size)
            scores = dot(kb[head, :size], qt[:, span])
            frame_of = (lax.broadcasted_iota(jnp.int32, (1, chunk), 1) + c * chunk) // per_frame
            low = jnp.where(frame_of >= boundary, boundary, 0) * per_frame
            high = (frame_of + 1) * per_frame
            key_ids = lax.broadcasted_iota(jnp.int32, (size, chunk), 0)
            scores = jnp.where((key_ids >= low) & (key_ids < high), scores, NEG_FILL)
            top = jnp.max(scores, axis=0, keepdims=True)
            prob = jnp.exp2((scores - top) * exp_scale)
            prob = prob * (1.0 / jnp.sum(prob, axis=0, keepdims=True))
            weights = prob.astype(BF)
            out_t = dot(vt[:, :size], weights).astype(BF)
            ob[head, span] = out_t.T
            g_t = gt[:, span]
            grad_dot = jnp.sum(g_t.astype(F32) * out_t.astype(F32), axis=0, keepdims=True)
            prob_grad = dot(vb[head, :size], g_t)
            score_grad = (prob * ((prob_grad - grad_dot) * score_scale)).astype(BF)
            dqb[head, span] = dot(kt[:, :size], score_grad).astype(BF).T
            dk_part = dot(score_grad, qb[head, span])
            dv_part = dot(weights, gb[head, span])
            if size == rows:
                dk_acc[...] = dk_part
                dv_acc[...] = dv_part
            else:
                dk_acc[:size] += dk_part
                dv_acc[:size] += dv_part
        dkb[head] = dk_acc[...].astype(BF)
        dvb[head] = dv_acc[...].astype(BF)

    outputs = ((ob, o_out), (dqb, dq_out), (dkb, dk_out), (dvb, dv_out))

    def scatter_out(index, head):
        src, dst = outputs[index]
        columns = lanes(me * heads + head, HS)

        def block(t):
            return src.at[head, pl.ds(pl.multiple_of(t * here, here), here)]

        over_t(lambda t: send(
            block(t), dst.at[:, columns], out_send.at[index], out_recv.at[index], at_t(t)
        ))
        pltpu.make_async_copy(block(me), dst.at[:, columns], out_recv.at[index]).start()

    def sum_over_cores():
        wait_bytes(codes.at[pl.ds(0, nt - 1)], small_recv.at[HOT])
        all_codes = jnp.concatenate([codes[t] for t in range(nt)], axis=1)
        code_rows = lax.broadcasted_iota(jnp.int32, (NC, rows), 0).astype(F32)
        hot = (code_rows == all_codes).astype(BF)
        for head in range(heads):
            blob[:, head * HS:(head + 1) * HS] = dot(hot, dqb[head])
        wait_bytes(cin.at[pl.ds(0, nt - 1)], small_recv.at[CT])
        total = cin[0]
        for t in range(1, nt):
            total += cin[t]
        blob[:, width:] = total
        small(blob, core_in, ARC, other_core)

    def sum_over_y():
        wait_bytes(core_in, small_recv.at[ARC])
        y_in[yy] = blob[...] + core_in[...]
        over_y(lambda y: small(y_in.at[yy], y_in.at[yy], ARY, at_y(y)))

    def sum_over_x():
        wait_bytes(y_in.at[pl.ds(0, ny - 1)], small_recv.at[ARY])
        total = y_in[0]
        for y in range(1, ny):
            total += y_in[y]
        x_in[xx] = total
        over_x(lambda x: small(x_in.at[xx], x_in.at[xx], ARX, at_x(x)))

    def share_sums():
        wait_bytes(x_in.at[pl.ds(0, nx - 1)], small_recv.at[ARX])
        total = x_in[0]
        for x in range(1, nx):
            total += x_in[x]
        half = (width + part) // 2
        sums[me] = jnp.concatenate([total[:, :half], total[:, half:]], axis=0).astype(BF)
        over_t(lambda t: small(sums.at[me], sums.at[me], FA, at_t(t)))

    inputs = ((k_ref, kb, 1), (cond, qb, 0), (v_ref, vb, 2), (g_ref, gb, 3))
    pieces = [(index, src, dst, head) for head in range(heads) for src, dst, index in inputs]
    results = [(index, head) for head in range(heads) for index in range(4)]
    steps = {
        "c": [condition], "y": [rows_over_y], "d": [rows_over_cores],
        "s": [add_cores, add_y, add_x, add_t],
        "t": [sum_over_cores, sum_over_y, sum_over_x, share_sums],
    }
    done = 0
    for step in ORDER:
        if step == "i":
            if pieces:
                scatter_in(*pieces.pop(0))
        elif step == "o":
            if results:
                scatter_out(*results.pop(0))
        elif step == "A":
            if done < heads:
                attend(done)
            done += 1
        elif step == "d":
            delta = rows_over_cores()
        elif step == "e":
            encode(delta)
        else:
            steps[step].pop(0)()

    wait_bytes(ge.at[:, pl.ds(0, (nt - 1) * part)], small_recv.at[GE])
    wait_bytes(sums.at[pl.ds(0, nt - 1)], small_recv.at[FA])
    for t in range(nt):
        got = sums[t].astype(F32)
        got = jnp.concatenate([got[:NC], got[NC:]], axis=1)
        ga[:, t * width:(t + 1) * width] = got[:, :width]
        gc[:, t * part:(t + 1) * part] = got[:, width:]
    ends = [
        pltpu.make_async_copy(src, dst, load.at[i])
        for i, (src, dst) in enumerate(((ge, ge_out), (ga, ga_out), (gc, gc_out)))
    ]
    for copy in ends:
        copy.start()
    for index, dst in enumerate((o_out, dq_out, dk_out, dv_out)):
        wait_bytes(dst, out_recv.at[index])
    sent = qb.at[:, pl.ds(0, rows - here)]
    for index in range(4):
        wait_bytes(sent, in_send.at[index])
        wait_bytes(sent, out_send.at[index])
    for index, view in (
        (LAM, prev),
        (AGX, wg.at[0, pl.ds(0, nx - 1), 0]),
        (AGY, wg.at[pl.ds(0, ny - 1), :, 0]),
        (AGC, wg.at[:, :, 0]),
        (HOT, codes.at[pl.ds(0, nt - 1)]),
        (RSC, rc),
        (ARC, core_in),
        (RSY, ry.at[pl.ds(0, ny - 1)]),
        (RSX, rx.at[pl.ds(0, nx - 1)]),
        (RST, rt.at[pl.ds(0, nt - 1)]),
        (GE, ge.at[:, pl.ds(0, (nt - 1) * part)]),
        (CT, cin.at[pl.ds(0, nt - 1)]),
        (ARY, y_in.at[pl.ds(0, ny - 1)]),
        (ARX, x_in.at[pl.ds(0, nx - 1)]),
        (FA, sums.at[pl.ds(0, nt - 1)]),
    ):
        wait_bytes(view, small_send.at[index])
    for copy in ends:
        copy.wait()


def keep(*refs):
    raw, done, held, sem_in, sem_out = refs[:7], refs[7:14], *refs[14:]
    stores = [pltpu.make_async_copy(raw[i], done[i], sem_out.at[i]) for i in range(6)]
    load = pltpu.make_async_copy(raw[6], held, sem_in)
    load.start()
    for copy in stores:
        copy.start()
    load.wait()
    done[6][...] = held[...].astype(F32)
    for copy in stores:
        copy.wait()


def per_device(
    ny, nx, nc, nt, chunk,
    queries, keys, values, out_grad, action_table, lam_tokens, enc_weight, codebook,
    action_codes, episode_start,
):
    shape = queries.shape
    here = shape[1] * shape[2]
    wide = shape[3]
    lam_width = lam_tokens.shape[3]
    heads = wide // HS // nt
    rows = here * nt
    part = lam_width // nt
    enc_rows = enc_weight.shape[0]
    vmem = pl.BlockSpec(memory_space=pltpu.VMEM)
    smem = pl.BlockSpec(memory_space=pltpu.SMEM)
    anywhere = pl.BlockSpec(memory_space=pl.ANY)
    head_block = pltpu.VMEM((heads, rows, HS), BF)
    turned = pltpu.VMEM((HS, rows), BF)
    flops = heads * rows * rows * HS * 2 * 6 + 2 * 2 * here * lam_width * lam_width
    flat = jax.ShapeDtypeStruct((here, wide), BF)
    results = pl.pallas_call(
        functools.partial(kernel, (ny, nx, nc, nt, chunk)),
        out_shape=(
            flat, flat, flat, flat,
            jax.ShapeDtypeStruct(action_table.shape, F32),
            jax.ShapeDtypeStruct(codebook.shape, F32),
            jax.ShapeDtypeStruct(enc_weight.shape, BF),
        ),
        in_specs=[anywhere] * 8 + [smem, smem],
        out_specs=[anywhere] * 7,
        scratch_shapes=[
            pltpu.VMEM((here, wide), BF),
            pltpu.VMEM(action_table.shape, F32),
            pltpu.VMEM((here, lam_width), BF),
            pltpu.VMEM(codebook.shape, F32),
            pltpu.VMEM((here, wide), BF),
            head_block, head_block, head_block, head_block,
            head_block, head_block, head_block, head_block,
            turned, turned, turned, turned,
            pltpu.VMEM((rows, HS), F32),
            pltpu.VMEM((rows, HS), F32),
            pltpu.VMEM((nt, 1, here), F32),
            pltpu.VMEM((here // 2, lam_width), BF),
            pltpu.VMEM((ny, nx, nc, enc_rows, lam_width), BF),
            pltpu.VMEM((nc, ny, nx, enc_rows, lam_width), BF),
            pltpu.VMEM((ny, nx, enc_rows, lam_width), BF),
            pltpu.VMEM((ny, nx, enc_rows, lam_width), BF),
            pltpu.VMEM((ny, nx, enc_rows, lam_width), BF),
            pltpu.VMEM((nx, enc_rows, lam_width), BF),
            pltpu.VMEM((nx, enc_rows, lam_width), BF),
            pltpu.VMEM((nt, enc_rows, part), BF),
            pltpu.VMEM((nt, enc_rows, part), BF),
            pltpu.VMEM((enc_rows, part), BF),
            pltpu.VMEM((enc_rows, lam_width), BF),
            pltpu.VMEM((nt, NC, part), F32),
            pltpu.VMEM((nt, NC, part), F32),
            pltpu.VMEM((NC, heads * HS + part), F32),
            pltpu.VMEM((NC, heads * HS + part), F32),
            pltpu.VMEM((ny, NC, heads * HS + part), F32),
            pltpu.VMEM((nx, NC, heads * HS + part), F32),
            pltpu.VMEM((nt, 2 * NC, (heads * HS + part) // 2), BF),
            pltpu.VMEM(action_table.shape, F32),
            pltpu.VMEM(codebook.shape, F32),
            pltpu.SemaphoreType.DMA((5,)),
            pltpu.SemaphoreType.DMA((4, heads)),
            pltpu.SemaphoreType.DMA((4,)),
            pltpu.SemaphoreType.DMA((4,)),
            pltpu.SemaphoreType.DMA((4,)),
            pltpu.SemaphoreType.DMA((16,)),
            pltpu.SemaphoreType.DMA((16,)),
        ],
        compiler_params=pltpu.CompilerParams(
            collective_id=0, has_side_effects=True, vmem_limit_bytes=32 * 2**20
        ),
        cost_estimate=pl.CostEstimate(
            flops=flops, bytes_accessed=8 * here * wide * 2, transcendentals=heads * rows * rows
        ),
    )(
        *(
            pltpu.with_memory_space_constraint(x, pltpu.HBM)
            for x in (
                queries.reshape(here, wide), keys.reshape(here, wide), values.reshape(here, wide),
                out_grad.reshape(here, wide), action_table, lam_tokens.reshape(here, lam_width),
                enc_weight, codebook,
            )
        ),
        action_codes, episode_start,
    )
    results = pl.pallas_call(
        keep,
        out_shape=tuple(jax.ShapeDtypeStruct(r.shape, r.dtype) for r in results[:6])
        + (jax.ShapeDtypeStruct(enc_weight.shape, F32),),
        in_specs=[anywhere] * 7,
        out_specs=[anywhere] * 6 + [vmem],
        compiler_params=pltpu.CompilerParams(vmem_limit_bytes=8 * 2**20),
        scratch_shapes=[
            pltpu.VMEM(enc_weight.shape, BF),
            pltpu.SemaphoreType.DMA,
            pltpu.SemaphoreType.DMA((6,)),
        ],
    )(*results)
    return tuple(r.reshape(shape) for r in results[:4]) + tuple(results[4:])


def solution(mesh, dims=(4, 4, 2), chunk=256):
    ny, nx, nc = dims
    nt = mesh.shape["tm"]
    frames = P("dp", "tm", None, None)
    return jax.shard_map(
        functools.partial(per_device, ny, nx, nc, nt, chunk),
        mesh=mesh,
        in_specs=(
            frames, frames, frames, frames, P(), frames, P("dp", None), P(), P("dp", "tm"), P("dp"),
        ),
        out_specs=(frames, frames, frames, frames, P(), P(), P("dp", None)),
        check_vma=False,
    )
```

```python
import functools
import math

import jax
import jax.numpy as jnp
from jax import lax
from jax.experimental import pallas as pl
from jax.experimental.pallas import tpu as pltpu
from jax.sharding import PartitionSpec as P

HS = 128
NC = 8
NEG_FILL = -1e30
ORDER = "iciyiidiieiisiiAoosiioosAoosooAtoototto"
MESH = pl.DeviceIdType.MESH
BF = jnp.bfloat16
F32 = jnp.float32


def dot(a, b):
    return jnp.dot(a, b, preferred_element_type=F32)


def wait_bytes(view, sem):
    pltpu.make_async_copy(view, view, sem).wait()


def kernel(
    sizes,
    q_hbm, k_ref, v_ref, g_ref, tab_hbm, lam_hbm, enc_hbm, book_hbm, code_hbm, start_ref,
    o_out, dq_out, dk_out, dv_out, ga_out, gc_out, ge_out,
    code_ref, q_ref, tab_ref, lam_ref, book_ref, cond, qb, kb, vb, gb, ob, dqb, dkb, dvb, kt, vt, qt, gt, dk_acc, dv_acc,
    codes, prev, wg, dw, rc, s1, ry, s2, rx, s3, rt, s4, ge,
    cterm, cin, blob, core_in, y_in, x_in, sums, ga, gc,
    load, in_recv, in_send, out_recv, out_send, small_recv, small_send,
):
    ny, nx, nc, nt, chunk = sizes
    heads = qb.shape[0]
    rows = qb.shape[1]
    here = rows // nt
    per_frame = here // 2
    width = heads * HS
    lam_width = lam_ref.shape[1]
    part = lam_width // nt
    enc_rows = enc_hbm.shape[0]
    dp = lax.axis_index("dp")
    me = lax.axis_index("tm")
    core = dp % nc
    xx = (dp // nc) % nx
    yy = dp // (nc * nx)

    def at_t(t):
        return (dp, t)

    def at_x(x):
        return ((yy * nx + x) * nc + core, me)

    def at_y(y):
        return ((y * nx + xx) * nc + core, me)

    other_core = ((yy * nx + xx) * nc + (nc - 1 - core), me)

    def over_t(fn):
        def body(i, carry):
            step = nt // 2 + (1 - 2 * (i % 2)) * ((i + 1) // 2)
            fn((me + step) % nt)
            return carry

        lax.fori_loop(0, nt - 1, body, 0)

    def over_x(fn):
        def body(i, carry):
            fn((xx + 1 + i) % nx)
            return carry

        lax.fori_loop(0, nx - 1, body, 0)

    def over_y(fn):
        def body(i, carry):
            fn((yy + 1 + i) % ny)
            return carry

        lax.fori_loop(0, ny - 1, body, 0)

    own_rows = wg.at[yy, xx, core]
    loads = [
        pltpu.make_async_copy(src, dst, load.at[i])
        for i, (src, dst) in enumerate((
            (enc_hbm, own_rows), (lam_hbm, lam_ref), (q_hbm, q_ref),
            (tab_hbm, tab_ref), (book_hbm, book_ref), (code_hbm, code_ref),
        ))
    ]
    for copy in loads:
        copy.start()

    barrier = pltpu.get_barrier_semaphore()

    def greet(device):
        pl.semaphore_signal(barrier, inc=1, device_id=device, device_id_type=MESH)

    over_t(lambda t: greet(at_t(t)))
    over_x(lambda x: greet(at_x(x)))
    over_y(lambda y: greet(at_y(y)))
    greet(other_core)
    pl.semaphore_wait(barrier, (nt - 1) + (nx - 1) + (ny - 1) + 1)

    def send(src, dst, sem_s, sem_r, device):
        pltpu.make_async_remote_copy(
            src_ref=src, dst_ref=dst, send_sem=sem_s, recv_sem=sem_r,
            device_id=device, device_id_type=MESH,
        ).start()

    LAM, AGX, AGY, AGC, HOT, RSC, RSY, RSX, RST, GE, CT, ARC, ARY, ARX, FA = range(15)

    def small(src, dst, index, device):
        send(src, dst, small_send.at[index], small_recv.at[index], device)

    def lanes(index, size):
        return pl.ds(pl.multiple_of(index * size, size), size)

    loads[0].wait()
    over_x(lambda x: small(own_rows, own_rows, AGX, at_x(x)))
    loads[1].wait()
    loads[5].wait()
    small(lam_ref.at[pl.ds(per_frame, per_frame)], prev, LAM, at_t((me + 1) % nt))
    code_a, code_b = code_ref[0, 0], code_ref[0, 1]
    boundary = start_ref[0]
    lane_code = jnp.where(
        lax.broadcasted_iota(jnp.int32, (1, here), 1) < per_frame, code_a, code_b
    )
    codes[me] = lane_code.astype(F32)
    over_t(lambda t: small(codes.at[me], codes.at[me], HOT, at_t(t)))

    mine = pl.ds(pl.multiple_of(me * here, here), here)

    def scatter_in(index, src, dst, head):
        def one(t):
            send(
                src.at[:, lanes(t * heads + head, HS)], dst.at[head, mine],
                in_send.at[index], in_recv.at[index, head], at_t(t),
            )

        over_t(one)
        pltpu.make_async_copy(
            src.at[:, lanes(me * heads + head, HS)], dst.at[head, mine], in_recv.at[index, head]
        ).start()

    def condition():
        for copy in loads[2:5]:
            copy.wait()
        table = tab_ref[...]
        code_ids = lax.broadcasted_iota(jnp.int32, table.shape, 0)
        for frame, code in ((0, code_a), (1, code_b)):
            offset = jnp.sum(jnp.where(code_ids == code, table, 0.0), axis=0, keepdims=True)
            span = pl.ds(frame * per_frame, per_frame)
            cond[span] = (q_ref[span].astype(F32) + offset).astype(BF)

    def rows_over_y():
        wait_bytes(wg.at[0, pl.ds(0, nx - 1), 0], small_recv.at[AGX])
        over_y(lambda y: small(wg.at[yy, :, core], wg.at[yy, :, core], AGY, at_y(y)))

    def rows_over_cores():
        wait_bytes(prev, small_recv.at[LAM])
        lam = lam_ref[...].astype(F32)
        before = jnp.where(me > 0, prev[...].astype(F32), 0.0)
        delta = jnp.concatenate(
            [lam[:per_frame] - before, lam[per_frame:] - lam[:per_frame]], axis=0
        ).astype(BF)
        wait_bytes(wg.at[pl.ds(0, ny - 1), :, 0], small_recv.at[AGY])
        small(wg.at[:, :, core], wg.at[:, :, core], AGC, other_core)
        return delta

    def encode(delta):
        delta_t = delta.T
        wait_bytes(wg.at[:, :, 0], small_recv.at[AGC])
        slab = lam_width // ny
        encoded = jnp.zeros((here, lam_width), F32)
        for y in range(ny):
            encoded += dot(delta[:, y * slab:(y + 1) * slab], wg[y].reshape(slab, lam_width))
        sig = jax.nn.sigmoid(encoded)
        act = encoded * sig
        slope = sig * (1.0 + encoded * (1.0 - sig))
        book = book_ref[...]
        book_ids = lax.broadcasted_iota(jnp.int32, book.shape, 0)
        term = jnp.zeros(book.shape, F32)
        graded = []
        for frame, code in ((0, code_a), (1, code_b)):
            span = slice(frame * per_frame, (frame + 1) * per_frame)
            pooled = jnp.sum(act[span], axis=0, keepdims=True) * (1.0 / per_frame)
            target = jnp.sum(jnp.where(book_ids == code, book, 0.0), axis=0, keepdims=True)
            frame_id = me * 2 + frame
            live = jnp.where((frame_id >= 1) & (frame_id != boundary), 1.0 / (2 * nt), 0.0)
            residual = (pooled - target) * live
            term -= jnp.where(book_ids == code, residual, 0.0)
            graded.append(residual * (1.0 / per_frame) * slope[span])
        encoded_grad = jnp.concatenate(graded, axis=0).astype(BF)
        for t in range(nt):
            cterm[t] = term[:, t * part:(t + 1) * part]
        cin[me] = cterm[me]
        over_t(lambda t: small(cterm.at[t], cin.at[me], CT, at_t(t)))
        for yx in range(ny * nx):
            lo = yx * nc * enc_rows
            piece = dot(delta_t[lo:lo + nc * enc_rows], encoded_grad).astype(BF)
            for c in range(nc):
                dw[c, yx // nx, yx % nx] = piece[c * enc_rows:(c + 1) * enc_rows]
        small(dw.at[nc - 1 - core], rc, RSC, other_core)

    def add_cores():
        wait_bytes(rc, small_recv.at[RSC])
        for y in range(ny):
            s1[y] = (dw[core, y].astype(F32) + rc[y].astype(F32)).astype(BF)
        over_y(lambda y: small(s1.at[y], ry.at[yy], RSY, at_y(y)))
        ry[yy] = s1[yy]

    def add_y():
        wait_bytes(ry.at[pl.ds(0, ny - 1)], small_recv.at[RSY])
        total = ry[0].astype(F32)
        for y in range(1, ny):
            total += ry[y].astype(F32)
        s2[...] = total.astype(BF)
        over_x(lambda x: small(s2.at[x], rx.at[xx], RSX, at_x(x)))
        rx[xx] = s2[xx]

    def add_x():
        wait_bytes(rx.at[pl.ds(0, nx - 1)], small_recv.at[RSX])
        total = rx[0].astype(F32)
        for x in range(1, nx):
            total += rx[x].astype(F32)
        total = total.astype(BF)
        for t in range(nt):
            s3[t] = total[:, t * part:(t + 1) * part]
        over_t(lambda t: small(s3.at[t], rt.at[me], RST, at_t(t)))
        rt[me] = s3[me]

    def add_t():
        wait_bytes(rt.at[pl.ds(0, nt - 1)], small_recv.at[RST])
        total = rt[0].astype(F32)
        for t in range(1, nt):
            total += rt[t].astype(F32)
        s4[...] = total.astype(BF)
        ge[:, lanes(me, part)] = s4[...]
        over_t(lambda t: small(s4, ge.at[:, lanes(me, part)], GE, at_t(t)))

    score_scale = 1.0 / math.sqrt(HS)
    exp_scale = score_scale * math.log2(math.e)

    def attend(head):
        for index, block in ((0, qb), (1, kb), (2, vb), (3, gb)):
            wait_bytes(block.at[head], in_recv.at[index, head])
        kt[...] = kb[head].T
        vt[...] = vb[head].T
        qt[...] = qb[head].T
        gt[...] = gb[head].T
        for c in reversed(range(rows // chunk)):
            size = (c + 1) * chunk
            span = slice(c * chunk, size)
            scores = dot(kb[head, :size], qt[:, span])
            frame_of = (lax.broadcasted_iota(jnp.int32, (1, chunk), 1) + c * chunk) // per_frame
            low = jnp.where(frame_of >= boundary, boundary, 0) * per_frame
            high = (frame_of + 1) * per_frame
            key_ids = lax.broadcasted_iota(jnp.int32, (size, chunk), 0)
            scores = jnp.where((key_ids >= low) & (key_ids < high), scores, NEG_FILL)
            top = jnp.max(scores, axis=0, keepdims=True)
            prob = jnp.exp2((scores - top) * exp_scale)
            prob = prob * (1.0 / jnp.sum(prob, axis=0, keepdims=True))
            weights = prob.astype(BF)
            out_t = dot(vt[:, :size], weights).astype(BF)
            ob[head, span] = out_t.T
            g_t = gt[:, span]
            grad_dot = jnp.sum(g_t.astype(F32) * out_t.astype(F32), axis=0, keepdims=True)
            prob_grad = dot(vb[head, :size], g_t)
            score_grad = (prob * ((prob_grad - grad_dot) * score_scale)).astype(BF)
            dqb[head, span] = dot(kt[:, :size], score_grad).astype(BF).T
            dk_part = dot(score_grad, qb[head, span])
            dv_part = dot(weights, gb[head, span])
            if size == rows:
                dk_acc[...] = dk_part
                dv_acc[...] = dv_part
            else:
                dk_acc[:size] += dk_part
                dv_acc[:size] += dv_part
        dkb[head] = dk_acc[...].astype(BF)
        dvb[head] = dv_acc[...].astype(BF)

    outputs = ((ob, o_out), (dqb, dq_out), (dkb, dk_out), (dvb, dv_out))

    def scatter_out(index, head):
        src, dst = outputs[index]
        columns = lanes(me * heads + head, HS)

        def block(t):
            return src.at[head, pl.ds(pl.multiple_of(t * here, here), here)]

        over_t(lambda t: send(
            block(t), dst.at[:, columns], out_send.at[index], out_recv.at[index], at_t(t)
        ))
        pltpu.make_async_copy(block(me), dst.at[:, columns], out_recv.at[index]).start()

    def sum_over_cores():
        wait_bytes(codes.at[pl.ds(0, nt - 1)], small_recv.at[HOT])
        all_codes = jnp.concatenate([codes[t] for t in range(nt)], axis=1)
        code_rows = lax.broadcasted_iota(jnp.int32, (NC, rows), 0).astype(F32)
        hot = (code_rows == all_codes).astype(BF)
        for head in range(heads):
            blob[:, head * HS:(head + 1) * HS] = dot(hot, dqb[head])
        wait_bytes(cin.at[pl.ds(0, nt - 1)], small_recv.at[CT])
        total = cin[0]
        for t in range(1, nt):
            total += cin[t]
        blob[:, width:] = total
        small(blob, core_in, ARC, other_core)

    def sum_over_y():
        wait_bytes(core_in, small_recv.at[ARC])
        y_in[yy] = blob[...] + core_in[...]
        over_y(lambda y: small(y_in.at[yy], y_in.at[yy], ARY, at_y(y)))

    def sum_over_x():
        wait_bytes(y_in.at[pl.ds(0, ny - 1)], small_recv.at[ARY])
        total = y_in[0]
        for y in range(1, ny):
            total += y_in[y]
        x_in[xx] = total
        over_x(lambda x: small(x_in.at[xx], x_in.at[xx], ARX, at_x(x)))

    def share_sums():
        wait_bytes(x_in.at[pl.ds(0, nx - 1)], small_recv.at[ARX])
        total = x_in[0]
        for x in range(1, nx):
            total += x_in[x]
        half = (width + part) // 2
        sums[me] = jnp.concatenate([total[:, :half], total[:, half:]], axis=0).astype(BF)
        over_t(lambda t: small(sums.at[me], sums.at[me], FA, at_t(t)))

    inputs = ((k_ref, kb, 1), (cond, qb, 0), (v_ref, vb, 2), (g_ref, gb, 3))
    pieces = [(index, src, dst, head) for head in range(heads) for src, dst, index in inputs]
    results = [(index, head) for head in range(heads) for index in range(4)]
    steps = {
        "c": [condition], "y": [rows_over_y], "d": [rows_over_cores],
        "s": [add_cores, add_y, add_x, add_t],
        "t": [sum_over_cores, sum_over_y, sum_over_x, share_sums],
    }
    done = 0
    for step in ORDER:
        if step == "i":
            if pieces:
                scatter_in(*pieces.pop(0))
        elif step == "o":
            if results:
                scatter_out(*results.pop(0))
        elif step == "A":
            if done < heads:
                attend(done)
            done += 1
        elif step == "d":
            delta = rows_over_cores()
        elif step == "e":
            encode(delta)
        else:
            steps[step].pop(0)()

    wait_bytes(ge.at[:, pl.ds(0, (nt - 1) * part)], small_recv.at[GE])
    wait_bytes(sums.at[pl.ds(0, nt - 1)], small_recv.at[FA])
    for t in range(nt):
        got = sums[t].astype(F32)
        got = jnp.concatenate([got[:NC], got[NC:]], axis=1)
        ga[:, t * width:(t + 1) * width] = got[:, :width]
        gc[:, t * part:(t + 1) * part] = got[:, width:]
    ends = [
        pltpu.make_async_copy(src, dst, load.at[i])
        for i, (src, dst) in enumerate(((ge, ge_out), (ga, ga_out), (gc, gc_out)))
    ]
    for copy in ends:
        copy.start()
    for index, dst in enumerate((o_out, dq_out, dk_out, dv_out)):
        wait_bytes(dst, out_recv.at[index])
    sent = qb.at[:, pl.ds(0, rows - here)]
    for index in range(4):
        wait_bytes(sent, in_send.at[index])
        wait_bytes(sent, out_send.at[index])
    for index, view in (
        (LAM, prev),
        (AGX, wg.at[0, pl.ds(0, nx - 1), 0]),
        (AGY, wg.at[pl.ds(0, ny - 1), :, 0]),
        (AGC, wg.at[:, :, 0]),
        (HOT, codes.at[pl.ds(0, nt - 1)]),
        (RSC, rc),
        (ARC, core_in),
        (RSY, ry.at[pl.ds(0, ny - 1)]),
        (RSX, rx.at[pl.ds(0, nx - 1)]),
        (RST, rt.at[pl.ds(0, nt - 1)]),
        (GE, ge.at[:, pl.ds(0, (nt - 1) * part)]),
        (CT, cin.at[pl.ds(0, nt - 1)]),
        (ARY, y_in.at[pl.ds(0, ny - 1)]),
        (ARX, x_in.at[pl.ds(0, nx - 1)]),
        (FA, sums.at[pl.ds(0, nt - 1)]),
    ):
        wait_bytes(view, small_send.at[index])
    for copy in ends:
        copy.wait()


def keep(*refs):
    raw, done, held, sem_in, sem_out = refs[:7], refs[7:14], *refs[14:]
    stores = [pltpu.make_async_copy(raw[i], done[i], sem_out.at[i]) for i in range(6)]
    load = pltpu.make_async_copy(raw[6], held, sem_in)
    load.start()
    for copy in stores:
        copy.start()
    load.wait()
    done[6][...] = held[...].astype(F32)
    for copy in stores:
        copy.wait()


def per_device(
    ny, nx, nc, nt, chunk,
    queries, keys, values, out_grad, action_table, lam_tokens, enc_weight, codebook,
    action_codes, episode_start,
):
    shape = queries.shape
    here = shape[1] * shape[2]
    wide = shape[3]
    lam_width = lam_tokens.shape[3]
    heads = wide // HS // nt
    rows = here * nt
    part = lam_width // nt
    enc_rows = enc_weight.shape[0]
    vmem = pl.BlockSpec(memory_space=pltpu.VMEM)
    smem = pl.BlockSpec(memory_space=pltpu.SMEM)
    anywhere = pl.BlockSpec(memory_space=pl.ANY)
    head_block = pltpu.VMEM((heads, rows, HS), BF)
    turned = pltpu.VMEM((HS, rows), BF)
    flops = heads * rows * rows * HS * 2 * 6 + 2 * 2 * here * lam_width * lam_width
    flat = jax.ShapeDtypeStruct((here, wide), BF)
    results = pl.pallas_call(
        functools.partial(kernel, (ny, nx, nc, nt, chunk)),
        out_shape=(
            flat, flat, flat, flat,
            jax.ShapeDtypeStruct(action_table.shape, F32),
            jax.ShapeDtypeStruct(codebook.shape, F32),
            jax.ShapeDtypeStruct(enc_weight.shape, BF),
        ),
        in_specs=[anywhere] * 9 + [smem],
        out_specs=[anywhere] * 7,
        scratch_shapes=[
            pltpu.SMEM(action_codes.shape, jnp.int32),
            pltpu.VMEM((here, wide), BF),
            pltpu.VMEM(action_table.shape, F32),
            pltpu.VMEM((here, lam_width), BF),
            pltpu.VMEM(codebook.shape, F32),
            pltpu.VMEM((here, wide), BF),
            head_block, head_block, head_block, head_block,
            head_block, head_block, head_block, head_block,
            turned, turned, turned, turned,
            pltpu.VMEM((rows, HS), F32),
            pltpu.VMEM((rows, HS), F32),
            pltpu.VMEM((nt, 1, here), F32),
            pltpu.VMEM((here // 2, lam_width), BF),
            pltpu.VMEM((ny, nx, nc, enc_rows, lam_width), BF),
            pltpu.VMEM((nc, ny, nx, enc_rows, lam_width), BF),
            pltpu.VMEM((ny, nx, enc_rows, lam_width), BF),
            pltpu.VMEM((ny, nx, enc_rows, lam_width), BF),
            pltpu.VMEM((ny, nx, enc_rows, lam_width), BF),
            pltpu.VMEM((nx, enc_rows, lam_width), BF),
            pltpu.VMEM((nx, enc_rows, lam_width), BF),
            pltpu.VMEM((nt, enc_rows, part), BF),
            pltpu.VMEM((nt, enc_rows, part), BF),
            pltpu.VMEM((enc_rows, part), BF),
            pltpu.VMEM((enc_rows, lam_width), BF),
            pltpu.VMEM((nt, NC, part), F32),
            pltpu.VMEM((nt, NC, part), F32),
            pltpu.VMEM((NC, heads * HS + part), F32),
            pltpu.VMEM((NC, heads * HS + part), F32),
            pltpu.VMEM((ny, NC, heads * HS + part), F32),
            pltpu.VMEM((nx, NC, heads * HS + part), F32),
            pltpu.VMEM((nt, 2 * NC, (heads * HS + part) // 2), BF),
            pltpu.VMEM(action_table.shape, F32),
            pltpu.VMEM(codebook.shape, F32),
            pltpu.SemaphoreType.DMA((6,)),
            pltpu.SemaphoreType.DMA((4, heads)),
            pltpu.SemaphoreType.DMA((4,)),
            pltpu.SemaphoreType.DMA((4,)),
            pltpu.SemaphoreType.DMA((4,)),
            pltpu.SemaphoreType.DMA((16,)),
            pltpu.SemaphoreType.DMA((16,)),
        ],
        compiler_params=pltpu.CompilerParams(
            collective_id=0, has_side_effects=True, vmem_limit_bytes=32 * 2**20
        ),
        cost_estimate=pl.CostEstimate(
            flops=flops, bytes_accessed=8 * here * wide * 2, transcendentals=heads * rows * rows
        ),
    )(
        *(
            pltpu.with_memory_space_constraint(x, pltpu.HBM)
            for x in (
                queries.reshape(here, wide), keys.reshape(here, wide), values.reshape(here, wide),
                out_grad.reshape(here, wide), action_table, lam_tokens.reshape(here, lam_width),
                enc_weight, codebook, action_codes,
            )
        ),
        episode_start,
    )
    results = pl.pallas_call(
        keep,
        out_shape=tuple(jax.ShapeDtypeStruct(r.shape, r.dtype) for r in results[:6])
        + (jax.ShapeDtypeStruct(enc_weight.shape, F32),),
        in_specs=[anywhere] * 7,
        out_specs=[anywhere] * 6 + [vmem],
        compiler_params=pltpu.CompilerParams(vmem_limit_bytes=8 * 2**20),
        scratch_shapes=[
            pltpu.VMEM(enc_weight.shape, BF),
            pltpu.SemaphoreType.DMA,
            pltpu.SemaphoreType.DMA((6,)),
        ],
    )(*results)
    return tuple(r.reshape(shape) for r in results[:4]) + tuple(results[4:])


def solution(mesh, dims=(4, 4, 2), chunk=256):
    ny, nx, nc = dims
    nt = mesh.shape["tm"]
    frames = P("dp", "tm", None, None)
    return jax.shard_map(
        functools.partial(per_device, ny, nx, nc, nt, chunk),
        mesh=mesh,
        in_specs=(
            frames, frames, frames, frames, P(), frames, P("dp", None), P(), P("dp", "tm"), P("dp"),
        ),
        out_specs=(frames, frames, frames, frames, P(), P(), P("dp", None)),
        check_vma=False,
    )
```
